256 devices in a mesh: batch: 8 (over y, core), proto: 32 (over z, x).
Axes of the slice: x: 4, y: 4, z: 8, core: 2. Of those that a mesh axis runs over, the one named last changes fastest.
Arguments:
- student_codes: bfloat16 [8192, 256], P(('batch', 'proto')), may hold values from -2.5 to 2.5
- teacher_codes: bfloat16 [8192, 256], P(('batch', 'proto')), may hold values from -2.5 to 2.5
- prototypes: float32 [256, 65536], P(None, 'proto'), may hold values from -48 to 48
Outputs:
- proto_grad: float32 [256, 65536], P('batch', 'proto')
- loss_rows: float32 [8192], P(('batch', 'proto'))
The draws below stay inside these ranges and needn't reach their ends.
All inputs are finite; a program needn't handle non-finite values.
Results may differ from the reference program's by a relative error of at most 0.0009.
The reference program's roundings to bfloat16 on the way (of `student_unit`, `teacher_unit`, `directions_low` and `score_grad`) count: a program that leaves them out, or rounds other values in their place, can miss the bound.
Values may be sent and summed in bfloat16 or wider, within the bound.
No kernel may reach another device: no remote copies, remote signals or barrier semaphores. Data moves between devices by JAX's collectives and lax.ppermute only.
A program may use at most 64 MiB of HBM per device.

```python
import math
import jax
import jax.numpy as jnp
from jax import lax

D = 256
CROPS = 1024
ITERS = 3
PROTOS = 65536
ALL_CROPS = 8192


def shared_table(key, center):
    return center + jax.random.truncated_normal(jax.random.fold_in(key, 101), -5.0, 5.0, (D, PROTOS), jnp.float32)


def shared_columns(key, center):
    table = shared_table(key, center)
    pool = jax.random.permutation(jax.random.fold_in(key, 102), PROTOS)[:16]
    group = jnp.arange(ALL_CROPS) // CROPS
    offset = jax.random.randint(jax.random.fold_in(key, 103), (ALL_CROPS,), 0, 4)
    slot = (2 * group + offset) % 16
    chosen = jnp.take(pool, slot)
    return jnp.take(table, chosen, axis=1).T


def mixed_codes(key, columns, strength_low, strength_high, jitter):
    strength = jnp.exp(jax.random.uniform(jax.random.fold_in(key, 7), (ALL_CROPS, 1), jnp.float32, jnp.log(strength_low), jnp.log(strength_high)))
    return ((strength * columns + jitter) / 16.0).astype(jnp.bfloat16)


def draw_student_codes(key, part):
    columns = shared_columns(key, 0.5)
    key = jax.random.fold_in(key, 1)
    jitter = jax.random.truncated_normal(key, -6.0, 6.0, (ALL_CROPS, D), jnp.float32)
    return mixed_codes(key, columns, 0.5, 2.0, jitter)


def draw_teacher_codes(key, part):
    columns = shared_columns(key, 0.5)
    key = jax.random.fold_in(key, 2)
    jitter = jax.random.truncated_normal(key, -6.0, 6.0, (ALL_CROPS, D), jnp.float32)
    return mixed_codes(key, columns, 1.0, 4.0, jitter)


def draw_prototypes(key, part):
    table = shared_table(key, 0.5)
    key = jax.random.fold_in(key, 3)
    column_gain = jnp.exp(jax.random.uniform(key, (1, PROTOS), jnp.float32, jnp.log(0.5), jnp.log(4.0)))
    return table * column_gain


def setup_inputs(seed: int = 0) -> dict:
    seeds = jax.random.split(jax.random.key(seed), 4)
    student_codes = draw_student_codes(jax.random.fold_in(seeds[3], 71), 0)
    teacher_codes = draw_teacher_codes(jax.random.fold_in(seeds[3], 71), 0)
    prototypes = draw_prototypes(jax.random.fold_in(seeds[3], 71), 0)
    return dict(student_codes=student_codes, teacher_codes=teacher_codes, prototypes=prototypes)


student_temp = 0.1
teacher_temp = 0.07
norm_eps = 1e-06

def unit_rows(values):
    values = values.astype(jnp.float32)
    return values * lax.rsqrt(lax.optimization_barrier(jnp.sum(values * values, axis=-1, keepdims=True)) + norm_eps)

def reference(student_codes, teacher_codes, prototypes):
    student_unit = unit_rows(student_codes).astype(jnp.bfloat16).astype(jnp.float32)
    teacher_unit = unit_rows(teacher_codes).astype(jnp.bfloat16).astype(jnp.float32)
    inverse_norm = lax.rsqrt(lax.optimization_barrier(jnp.sum(prototypes * prototypes, axis=0)) + norm_eps)
    directions = prototypes * inverse_norm[None, :]
    directions_low = directions.astype(jnp.bfloat16)
    code_width, proto_count = prototypes.shape
    row_total = student_codes.shape[0]
    block_size = math.gcd(proto_count, 4096)
    blocked = directions_low.reshape(code_width, proto_count // block_size, block_size).transpose(1, 0, 2)

    def first_pass(proto_piece):
        proto_piece = proto_piece.astype(jnp.float32)
        teacher_scores = jnp.dot(teacher_unit, proto_piece, precision=lax.Precision.HIGHEST)
        student_scores = jnp.dot(student_unit, proto_piece, precision=lax.Precision.HIGHEST)
        return (jnp.exp(teacher_scores / teacher_temp), lax.optimization_barrier(jnp.sum(jnp.exp(student_scores / student_temp), axis=1)))
    weights, partial_totals = lax.map(first_pass, blocked)
    student_total = lax.optimization_barrier(jnp.sum(partial_totals, axis=0))
    row_scale = jnp.ones((row_total,), jnp.float32)
    column_scale = jnp.ones((proto_count // block_size, block_size), jnp.float32)
    for iteration in range(ITERS):
        column_scale = 1.0 / jnp.einsum('nbk,b->nk', weights, row_scale, precision=lax.Precision.HIGHEST)
        row_scale = 1.0 / jnp.einsum('nbk,nk->b', weights, column_scale, precision=lax.Precision.HIGHEST)

    def second_pass(inputs):
        proto_piece, weight_block, column_block = inputs
        proto_piece = proto_piece.astype(jnp.float32)
        student_scores = jnp.dot(student_unit, proto_piece, precision=lax.Precision.HIGHEST)
        targets = row_scale[:, None] * weight_block * column_block[None, :]
        student_prob = jnp.exp(student_scores / student_temp) / student_total[:, None]
        cross_sum = lax.optimization_barrier(jnp.sum(targets * student_scores, axis=1))
        score_grad = ((student_prob - targets) / (student_temp * row_total)).astype(jnp.bfloat16)
        grad_block = jnp.dot(student_unit.T, score_grad.astype(jnp.float32), precision=lax.Precision.HIGHEST)
        return (cross_sum, grad_block)
    cross_parts, grad_blocks = lax.map(second_pass, (blocked, weights, column_scale))
    cross_sum = lax.optimization_barrier(jnp.sum(cross_parts, axis=0))
    loss_rows = jnp.log(student_total) - cross_sum / student_temp
    grad_direction = grad_blocks.transpose(1, 0, 2).reshape(code_width, proto_count)
    radial = lax.optimization_barrier(jnp.sum(directions * grad_direction, axis=0))
    proto_grad = (grad_direction - directions * radial[None, :]) * inverse_norm[None, :]
    return (proto_grad, loss_rows)
```

```python
import jax
import jax.numpy as jnp
from jax import lax
from jax.sharding import Mesh, PartitionSpec as P

ITERS = 3

student_temp = 0.1
teacher_temp = 0.07
norm_eps = 1e-06

BATCH = ("y", "core")
PROTO = ("z", "x")


def unit_rows(values):
    values = values.astype(jnp.float32)
    return values * lax.rsqrt(jnp.sum(values * values, axis=-1, keepdims=True) + norm_eps)


def contract_rows(left_codes, right_grad):
    return lax.dot_general(
        left_codes, right_grad, (((0,), (0,)), ((), ())), preferred_element_type=jnp.float32
    )


def share(value, axes, count):
    copies = jnp.broadcast_to(value[None], (count,) + value.shape)
    return lax.all_to_all(copies, axes, 0, 0, tiled=True)


def total_over(value, axes, count):
    parts = share(value.reshape(-1, 128), axes, count)
    return jnp.sum(parts, axis=0).reshape(value.shape)


def scatter_sum(value):
    core = lax.axis_index("core")
    rows = value.shape[0] // 8
    blocks = value.reshape(4, 2, rows, value.shape[1])
    kept = lax.dynamic_index_in_dim(blocks, core, 1, False)
    other = lax.dynamic_index_in_dim(blocks, 1 - core, 1, False)
    pair = kept + lax.ppermute(other, "core", [(0, 1), (1, 0)])
    place = lax.axis_index("y")
    total = lax.dynamic_index_in_dim(pair, place, 0, False)
    for step in (2, 1, 3):
        block = lax.dynamic_index_in_dim(pair, (place + step) % 4, 0, False)
        total = total + lax.ppermute(block, "y", [(i, (i + step) % 4) for i in range(4)])
    return total


def on_device(student_codes, teacher_codes, prototypes):
    own_rows = student_codes.shape[0]
    codes = share(jnp.concatenate([teacher_codes, student_codes]), PROTO, 32)
    teacher_unit = unit_rows(codes[:, :own_rows].reshape(-1, codes.shape[-1])).astype(jnp.bfloat16)
    student_unit = unit_rows(codes[:, own_rows:].reshape(-1, codes.shape[-1])).astype(jnp.bfloat16)
    inverse_norm = lax.rsqrt(jnp.sum(prototypes * prototypes, axis=0) + norm_eps)
    directions = prototypes * inverse_norm[None, :]
    directions_low = directions.astype(jnp.bfloat16)
    teacher_scores = jnp.dot(teacher_unit, directions_low, preferred_element_type=jnp.float32)
    weights = jnp.exp(teacher_scores * (1.0 / teacher_temp))
    student_scores = jnp.dot(student_unit, directions_low, preferred_element_type=jnp.float32)
    student_exp = jnp.exp(student_scores * (1.0 / student_temp))
    partial_total = jnp.sum(student_exp, axis=1)
    column_mass = jnp.sum(weights, axis=0)
    for iteration in range(ITERS):
        column_scale = 1.0 / total_over(column_mass, BATCH, 8)
        scaled = weights * column_scale[None, :]
        row_mass = jnp.sum(scaled, axis=1)
        if iteration < ITERS - 1:
            row_scale = 1.0 / total_over(row_mass, PROTO, 32)
            column_mass = jnp.sum(weights * row_scale[:, None], axis=0)
    partial_cross = jnp.sum(scaled * student_scores, axis=1)
    row_mass, student_total, cross = jnp.split(
        total_over(jnp.concatenate([row_mass, partial_total, partial_cross]), PROTO, 32), 3
    )
    row_scale = 1.0 / row_mass
    row_total = student_unit.shape[0] * 8
    factor = 1.0 / (student_temp * row_total)
    score_grad = (
        student_exp * (factor / student_total)[:, None] - scaled * (factor * row_scale)[:, None]
    ).astype(jnp.bfloat16)
    loss_all = jnp.log(student_total) - cross * row_scale * (1.0 / student_temp)
    place = lax.axis_index(PROTO)
    loss_rows = lax.dynamic_slice_in_dim(loss_all, place * own_rows, own_rows, 0)
    grad_terms = contract_rows(student_unit, score_grad)
    radial = jnp.sum(directions * grad_terms, axis=0)
    full_grad = (grad_terms - directions * radial[None, :]) * inverse_norm[None, :]
    return (scatter_sum(full_grad), loss_rows)


def solution(mesh):
    fine = Mesh(mesh.devices.reshape(4, 2, 8, 4), BATCH + PROTO)
    rows = P(BATCH + PROTO, None)
    return jax.shard_map(
        on_device,
        mesh=fine,
        in_specs=(rows, rows, P(None, PROTO)),
        out_specs=(P(BATCH, PROTO), P(BATCH + PROTO)),
        check_vma=False,
    )
```

```python
import functools

import jax
import jax.numpy as jnp
from jax import lax
from jax.experimental import pallas as pl
from jax.experimental.pallas import tpu as pltpu
from jax.sharding import Mesh, PartitionSpec as P

ITERS = 3

student_temp = 0.1
teacher_temp = 0.07
norm_eps = 1e-06

BATCH = ("y", "core")
PROTO = ("z", "x")
BATCHES = 8
PROTOS = 32
ROWS = 1024
COLS = 2048
WIDTH = 256
LANES = 128
ROW_TILES = ROWS // LANES
COL_TILES = COLS // LANES
CHUNK = 256
f32 = jnp.float32
bf16 = jnp.bfloat16


def unit_rows(values):
    values = values.astype(f32)
    return values * lax.rsqrt(jnp.sum(values * values, axis=-1, keepdims=True) + norm_eps)


def row_of_lane_sums(parts_ref, out_row, pieces=ROW_TILES):
    for g in range(pieces):
        block = parts_ref[pl.ds(g * LANES, LANES), :]
        out_row(g, jnp.sum(block.T, axis=0, keepdims=True))


def column_of_row(row, out_ref):
    for g in range(ROW_TILES):
        out_ref[pl.ds(g * LANES, LANES), :] = jnp.broadcast_to(row[g : g + 1, :], (LANES, LANES)).T


def spread_columns(column_mass, pay_ref):
    row = jnp.concatenate([column_mass[:, t * LANES : (t + 1) * LANES] for t in range(COL_TILES)], axis=0)
    for k in range(BATCHES):
        pay_ref[k] = row


def norm_kernel(proto_ref, low_ref, inverse_ref):
    for j in range(0, COLS, CHUNK):
        cols = pl.ds(j, CHUNK)
        piece = proto_ref[:, cols]
        inverse = lax.rsqrt(jnp.sum(piece * piece, axis=0, keepdims=True) + norm_eps)
        inverse_ref[:, cols] = inverse
        low_ref[:, cols] = (piece * inverse).astype(bf16)


def teacher_kernel(codes_ref, low_ref, weights_ref, pay_ref, unit_ref, mass_ref):
    for i in range(0, PROTOS, 4):
        piece = codes_ref[i : i + 4, 0:32, :].reshape(LANES, WIDTH)
        unit_ref[pl.ds(i * 32, LANES), :] = unit_rows(piece).astype(bf16)

    @pl.loop(0, COLS // CHUNK)
    def _(j):
        cols = pl.ds(pl.multiple_of(j * CHUNK, CHUNK), CHUNK)
        low = low_ref[:, cols]
        mass = jnp.zeros((8, CHUNK), f32)
        for i in range(0, ROWS, 256):
            rows = pl.ds(i, 256)
            scores = jnp.dot(unit_ref[rows, :], low, preferred_element_type=f32)
            weights = jnp.exp(scores * (1.0 / teacher_temp))
            weights_ref[rows, cols] = weights
            mass = mass + jnp.sum(weights.reshape(32, 8, CHUNK), axis=0)
        mass_ref[:, cols] = jnp.sum(mass, axis=0, keepdims=True)

    spread_columns(mass_ref[...], pay_ref)


def student_kernel(codes_ref, low_ref, scores_ref, exp_ref, unit_t_ref, total_ref, unit_ref, parts_ref):
    for i in range(0, PROTOS, 4):
        piece = codes_ref[i : i + 4, 32:64, :].reshape(LANES, WIDTH)
        unit = unit_rows(piece)
        unit_ref[pl.ds(i * 32, LANES), :] = unit.astype(bf16)
        unit_t_ref[:, pl.ds(i * 32, LANES)] = unit.T.astype(bf16)
    parts_ref[...] = jnp.zeros_like(parts_ref)

    @pl.loop(0, COLS // CHUNK)
    def _(j):
        cols = pl.ds(pl.multiple_of(j * CHUNK, CHUNK), CHUNK)
        low = low_ref[:, cols]
        for i in range(0, ROWS, 256):
            rows = pl.ds(i, 256)
            scores = jnp.dot(unit_ref[rows, :], low, preferred_element_type=f32)
            scores_ref[rows, cols] = scores
            grown = jnp.exp(scores * (1.0 / student_temp))
            exp_ref[rows, cols] = grown
            parts_ref[rows, :] += grown[:, :LANES] + grown[:, LANES:]

    def put(g, row):
        total_ref[g : g + 1, :] = row

    row_of_lane_sums(parts_ref, put)


def scaled_rows(column, weights_ref, parts_ref, scores_ref=None, cross_ref=None):
    scale = [jnp.broadcast_to(column[t : t + 1, :], (8, LANES)) for t in range(COL_TILES)]

    @pl.loop(0, ROWS // 32)
    def _(i):
        for k in range(4):
            rows = pl.ds(pl.multiple_of(i * 32 + k * 8, 8), 8)
            mass = cross = None
            for t in range(COL_TILES):
                cols = pl.ds(t * LANES, LANES)
                term = weights_ref[rows, cols] * scale[t]
                mass = term if mass is None else mass + term
                if scores_ref is not None:
                    term = term * scores_ref[rows, cols]
                    cross = term if cross is None else cross + term
            parts_ref[rows, :] = mass
            if scores_ref is not None:
                cross_ref[rows, :] = cross


def row_kernel(mass_ref, weights_ref, pay_ref, parts_ref):
    column = 1.0 / jnp.sum(mass_ref[...], axis=0)
    scaled_rows(column, weights_ref, parts_ref)

    def put(g, row):
        for k in range(PROTOS):
            pay_ref[k, g : g + 1, :] = row

    row_of_lane_sums(parts_ref, put)


def last_row_kernel(mass_ref, weights_ref, scores_ref, total_ref, pay_ref, column_ref, parts_ref, cross_ref, row_ref):
    column = 1.0 / jnp.sum(mass_ref[...], axis=0)
    column_ref[...] = column
    scaled_rows(column, weights_ref, parts_ref, scores_ref, cross_ref)

    def put_mass(g, row):
        row_ref[g : g + 1, :] = row

    def put_cross(g, row):
        row_ref[16 + g : 17 + g, :] = row

    row_of_lane_sums(parts_ref, put_mass)
    row_of_lane_sums(cross_ref, put_cross)
    row_ref[8:16, :] = total_ref[...]
    row = row_ref[...]
    for k in range(PROTOS):
        pay_ref[k] = row


def column_kernel(mass_ref, weights_ref, pay_ref, scale_ref, sums_ref):
    column_of_row(1.0 / jnp.sum(mass_ref[...], axis=0), scale_ref)

    def step(i, sums):
        sums = list(sums)
        for k in range(2):
            rows = pl.ds(pl.multiple_of(i * 16 + k * 8, 8), 8)
            scale = scale_ref[rows, :]
            for t in range(COL_TILES):
                sums[t] = sums[t] + weights_ref[rows, pl.ds(t * LANES, LANES)] * scale
        return tuple(sums)

    sums = lax.fori_loop(0, ROWS // 16, step, tuple(jnp.zeros((8, LANES), f32) for _ in range(COL_TILES)))
    for t in range(COL_TILES):
        sums_ref[t : t + 1, :] = jnp.sum(sums[t], axis=0, keepdims=True)
    row = sums_ref[...]
    for k in range(BATCHES):
        pay_ref[k] = row


def grad_kernel(
    mass_ref, weights_ref, exp_ref, column_ref, unit_t_ref, proto_ref, inverse_ref, grad_ref, loss_ref, prob_ref, target_ref
):
    sums = jnp.sum(mass_ref[...], axis=0)
    row_scale = 1.0 / sums[0:8, :]
    total = sums[8:16, :]
    loss_ref[...] = jnp.log(total) - sums[16:24, :] * row_scale * (1.0 / student_temp)
    factor = 1.0 / (student_temp * ROWS * BATCHES)
    column_of_row(factor / total, prob_ref)
    column_of_row(factor * row_scale, target_ref)
    for j in range(COLS // CHUNK):
        cols = pl.ds(j * CHUNK, CHUNK)
        pieces = []
        for t in range(2):
            part = pl.ds(j * CHUNK + t * LANES, LANES)
            scale = column_ref[2 * j + t : 2 * j + t + 1, :]
            pieces.append(
                (exp_ref[:, part] * prob_ref[...] - weights_ref[:, part] * scale * target_ref[...]).astype(bf16)
            )
        score_grad = jnp.concatenate(pieces, axis=1)
        grad = jnp.dot(unit_t_ref[...], score_grad, preferred_element_type=f32)
        inverse = inverse_ref[:, cols]
        directions = proto_ref[:, cols] * inverse
        radial = jnp.sum(directions * grad, axis=0, keepdims=True)
        grad_ref[:, cols] = (grad - directions * radial) * inverse


def call(kernel, outs, scratch, ops, flops=0, elements=ROWS * COLS, inside=()):
    def shape(out):
        dims, dtype, kept = out
        return pltpu.VMEM(dims, dtype) if kept else jax.ShapeDtypeStruct(dims, dtype)

    def run(*operands):
        placed = [
            pltpu.with_memory_space_constraint(x, pltpu.VMEM) if i in inside else x for i, x in enumerate(operands)
        ]
        return pl.pallas_call(
            kernel,
            out_shape=[shape(o) for o in outs],
            in_specs=[pl.BlockSpec(memory_space=pltpu.VMEM)] * ops,
            out_specs=[pl.BlockSpec(memory_space=pltpu.VMEM)] * len(outs),
            scratch_shapes=scratch,
            compiler_params=pltpu.CompilerParams(vmem_limit_bytes=12 * 2**20),
            cost_estimate=pl.CostEstimate(flops=flops, bytes_accessed=4 * elements, transcendentals=0),
        )(*placed)

    return run


def share(value, axes, count):
    return lax.all_to_all(value, axes, 0, 0, tiled=True)


def scatter_sum(value):
    core = lax.axis_index("core")
    rows = value.shape[0] // 8
    blocks = value.reshape(4, 2, rows, value.shape[1])
    kept = lax.dynamic_index_in_dim(blocks, core, 1, False)
    other = lax.dynamic_index_in_dim(blocks, 1 - core, 1, False)
    pair = kept + lax.ppermute(other, "core", [(0, 1), (1, 0)])
    place = lax.axis_index("y")
    total = lax.dynamic_index_in_dim(pair, place, 0, False)
    for step in (2, 1, 3):
        block = lax.dynamic_index_in_dim(pair, (place + step) % 4, 0, False)
        total = total + lax.ppermute(block, "y", [(i, (i + step) % 4) for i in range(4)])
    return total


def on_device(student_codes, teacher_codes, prototypes):
    own_rows = student_codes.shape[0]
    mine = jnp.concatenate([teacher_codes, student_codes])
    codes = share(jnp.broadcast_to(mine[None], (PROTOS,) + mine.shape), PROTO, PROTOS)
    low, inverse = call(
        norm_kernel, [((WIDTH, COLS), bf16, True), ((1, COLS), f32, False)], [], 1, elements=WIDTH * COLS * 2
    )(prototypes)
    big = ROWS * COLS
    weights, pay = call(
        teacher_kernel,
        [((ROWS, COLS), f32, True), ((BATCHES, COL_TILES, LANES), f32, False)],
        [pltpu.VMEM((ROWS, WIDTH), bf16), pltpu.VMEM((1, COLS), f32)],
        2,
        flops=2 * big * WIDTH,
        inside=(1,),
    )(codes, low)
    scores, grown, unit_t, total = call(
        student_kernel,
        [((ROWS, COLS), f32, True), ((ROWS, COLS), f32, True), ((WIDTH, ROWS), bf16, True), ((ROW_TILES, LANES), f32, False)],
        [pltpu.VMEM((ROWS, WIDTH), bf16), pltpu.VMEM((ROWS, LANES), f32)],
        2,
        flops=2 * big * WIDTH,
        elements=2 * big,
        inside=(1,),
    )(codes, low)
    for iteration in range(ITERS - 1):
        (pay,) = call(
            row_kernel, [((PROTOS, ROW_TILES, LANES), f32, False)], [pltpu.VMEM((ROWS, LANES), f32)], 2, inside=(1,)
        )(share(pay, BATCH, BATCHES), weights)
        (pay,) = call(
            column_kernel,
            [((BATCHES, COL_TILES, LANES), f32, False)],
            [pltpu.VMEM((ROWS, LANES), f32), pltpu.VMEM((COL_TILES, LANES), f32)],
            2,
            inside=(1,),
        )(share(pay, PROTO, PROTOS), weights)
    pay, column = call(
        last_row_kernel,
        [((PROTOS, 3 * ROW_TILES, LANES), f32, False), ((COL_TILES, LANES), f32, False)],
        [pltpu.VMEM((ROWS, LANES), f32), pltpu.VMEM((ROWS, LANES), f32), pltpu.VMEM((3 * ROW_TILES, LANES), f32)],
        4,
        elements=2 * big,
        inside=(1, 2),
    )(share(pay, BATCH, BATCHES), weights, scores, total)
    grad, loss_all = call(
        grad_kernel,
        [((WIDTH, COLS), f32, True), ((ROW_TILES, LANES), f32, False)],
        [pltpu.VMEM((ROWS, LANES), f32), pltpu.VMEM((ROWS, LANES), f32)],
        7,
        flops=2 * big * WIDTH,
        elements=2 * big,
        inside=(1, 2, 4),
    )(share(pay, PROTO, PROTOS), weights, grown, column, unit_t, prototypes, inverse)
    place = lax.axis_index(PROTO)
    loss_rows = lax.dynamic_slice_in_dim(loss_all.reshape(ROWS), place * own_rows, own_rows, 0)
    return (scatter_sum(grad), loss_rows)


def solution(mesh):
    fine = Mesh(mesh.devices.reshape(4, 2, 8, 4), BATCH + PROTO)
    rows = P(BATCH + PROTO, None)
    return jax.shard_map(
        on_device,
        mesh=fine,
        in_specs=(rows, rows, P(None, PROTO)),
        out_specs=(P(BATCH, PROTO), P(BATCH + PROTO)),
        check_vma=False,
    )
```

```python
import functools

import jax
import jax.numpy as jnp
from jax import lax
from jax.experimental import pallas as pl
from jax.experimental.pallas import tpu as pltpu
from jax.sharding import Mesh, PartitionSpec as P

ITERS = 3

student_temp = 0.1
teacher_temp = 0.07
norm_eps = 1e-06

BATCH = ("y", "core")
PROTO = ("z", "x")
BATCHES = 8
PROTOS = 32
ROWS = 1024
COLS = 2048
WIDTH = 256
LANES = 128
ROW_TILES = ROWS // LANES
COL_TILES = COLS // LANES
CHUNK = 256
f32 = jnp.float32
bf16 = jnp.bfloat16


def unit_rows(values):
    values = values.astype(f32)
    return values * lax.rsqrt(jnp.sum(values * values, axis=-1, keepdims=True) + norm_eps)


def row_of_lane_sums(parts_ref, out_row, pieces=ROW_TILES):
    for g in range(pieces):
        block = parts_ref[pl.ds(g * LANES, LANES), :]
        out_row(g, jnp.sum(block.T, axis=0, keepdims=True))


def column_of_row(row, out_ref):
    for g in range(ROW_TILES):
        out_ref[pl.ds(g * LANES, LANES), :] = jnp.broadcast_to(row[g : g + 1, :], (LANES, LANES)).T


def spread_columns(column_mass, pay_ref):
    row = jnp.concatenate([column_mass[:, t * LANES : (t + 1) * LANES] for t in range(COL_TILES)], axis=0)
    for k in range(BATCHES):
        pay_ref[k] = row


def block_place(q):
    step = lax.rem(q // 2 - lax.axis_index("y") + 4, 4)
    return jnp.where(lax.axis_index("core") == q % 2, 0, 4) + step


def block_rows(p):
    row = lax.rem(lax.axis_index("y") + p % 4, 4)
    core = lax.axis_index("core")
    return 2 * row + (core if p < 4 else 1 - core)


def copy_kernel(teacher_ref, student_ref, pay_ref):
    teacher, student = teacher_ref[...], student_ref[...]
    for k in range(PROTOS):
        pay_ref[k, 0:32, :] = teacher
        pay_ref[k, 32:64, :] = student


def score_kernel(
    codes_ref,
    proto_ref,
    weights_ref,
    scores_ref,
    exp_ref,
    unit_t_ref,
    total_ref,
    inverse_ref,
    pay_ref,
    teacher_ref,
    student_ref,
    mass_ref,
    parts_ref,
):
    place = [pl.multiple_of(block_place(q) * 32, 32) for q in range(8)]
    for i in range(0, PROTOS, 4):
        rows = pl.ds(i * 32, LANES)
        teacher_ref[rows, :] = unit_rows(codes_ref[i : i + 4, 0:32, :].reshape(LANES, WIDTH)).astype(bf16)
        unit = unit_rows(codes_ref[i : i + 4, 32:64, :].reshape(LANES, WIDTH))
        student_ref[rows, :] = unit.astype(bf16)
        turned = unit.T.astype(bf16)
        for q in range(8):
            unit_t_ref[pl.ds(place[q], 32), rows] = turned[q * 32 : q * 32 + 32, :]
    parts_ref[...] = jnp.zeros_like(parts_ref)

    @pl.loop(0, COLS // CHUNK)
    def _(j):
        cols = pl.ds(pl.multiple_of(j * CHUNK, CHUNK), CHUNK)
        piece = proto_ref[:, cols]
        inverse = lax.rsqrt(jnp.sum(piece * piece, axis=0, keepdims=True) + norm_eps)
        inverse_ref[:, cols] = inverse
        low = (piece * inverse).astype(bf16)
        mass = jnp.zeros((8, CHUNK), f32)
        for i in range(0, ROWS, 256):
            rows = pl.ds(i, 256)
            scores = jnp.dot(teacher_ref[rows, :], low, preferred_element_type=f32)
            weights = jnp.exp(scores * (1.0 / teacher_temp))
            weights_ref[rows, cols] = weights
            mass = mass + jnp.sum(weights.reshape(32, 8, CHUNK), axis=0)
        mass_ref[:, cols] = jnp.sum(mass, axis=0, keepdims=True)
        for i in range(0, ROWS, 256):
            rows = pl.ds(i, 256)
            scores = jnp.dot(student_ref[rows, :], low, preferred_element_type=f32)
            scores_ref[rows, cols] = scores
            grown = jnp.exp(scores * (1.0 / student_temp))
            exp_ref[rows, cols] = grown
            parts_ref[rows, :] += grown[:, :LANES] + grown[:, LANES:]

    spread_columns(mass_ref[...], pay_ref)

    def put(g, row):
        total_ref[g : g + 1, :] = row

    row_of_lane_sums(parts_ref, put)


def scaled_rows(column, weights_ref, parts_ref, scores_ref=None, cross_ref=None):
    scale = [jnp.broadcast_to(column[t : t + 1, :], (8, LANES)) for t in range(COL_TILES)]

    @pl.loop(0, ROWS // 32)
    def _(i):
        for k in range(4):
            rows = pl.ds(pl.multiple_of(i * 32 + k * 8, 8), 8)
            mass = cross = None
            for t in range(COL_TILES):
                cols = pl.ds(t * LANES, LANES)
                term = weights_ref[rows, cols] * scale[t]
                mass = term if mass is None else mass + term
                if scores_ref is not None:
                    term = term * scores_ref[rows, cols]
                    cross = term if cross is None else cross + term
            parts_ref[rows, :] = mass
            if scores_ref is not None:
                cross_ref[rows, :] = cross


def row_kernel(mass_ref, weights_ref, pay_ref, parts_ref):
    column = 1.0 / jnp.sum(mass_ref[...], axis=0)
    scaled_rows(column, weights_ref, parts_ref)

    def put(g, row):
        for k in range(PROTOS):
            pay_ref[k, g : g + 1, :] = row

    row_of_lane_sums(parts_ref, put)


def last_row_kernel(mass_ref, weights_ref, scores_ref, total_ref, pay_ref, column_ref, parts_ref, cross_ref, row_ref):
    column = 1.0 / jnp.sum(mass_ref[...], axis=0)
    column_ref[...] = column
    scaled_rows(column, weights_ref, parts_ref, scores_ref, cross_ref)

    def put_mass(g, row):
        row_ref[g : g + 1, :] = row

    def put_cross(g, row):
        row_ref[16 + g : 17 + g, :] = row

    row_of_lane_sums(parts_ref, put_mass)
    row_of_lane_sums(cross_ref, put_cross)
    row_ref[8:16, :] = total_ref[...]
    row = row_ref[...]
    for k in range(PROTOS):
        pay_ref[k] = row


def column_kernel(mass_ref, weights_ref, pay_ref, scale_ref, sums_ref):
    column_of_row(1.0 / jnp.sum(mass_ref[...], axis=0), scale_ref)

    def step(i, sums):
        sums = list(sums)
        for k in range(2):
            rows = pl.ds(pl.multiple_of(i * 16 + k * 8, 8), 8)
            scale = scale_ref[rows, :]
            for t in range(COL_TILES):
                sums[t] = sums[t] + weights_ref[rows, pl.ds(t * LANES, LANES)] * scale
        return tuple(sums)

    sums = lax.fori_loop(0, ROWS // 16, step, tuple(jnp.zeros((8, LANES), f32) for _ in range(COL_TILES)))
    for t in range(COL_TILES):
        sums_ref[t : t + 1, :] = jnp.sum(sums[t], axis=0, keepdims=True)
    row = sums_ref[...]
    for k in range(BATCHES):
        pay_ref[k] = row


def grad_kernel(
    mass_ref,
    weights_ref,
    exp_ref,
    column_ref,
    unit_t_ref,
    proto_ref,
    inverse_ref,
    kept_ref,
    sent_ref,
    own_ref,
    prob_ref,
    target_ref,
    loss_ref,
):
    sums = jnp.sum(mass_ref[...], axis=0)
    row_scale = 1.0 / sums[0:8, :]
    total = sums[8:16, :]
    loss_ref[...] = jnp.log(total) - sums[16:24, :] * row_scale * (1.0 / student_temp)
    place = lax.axis_index("z") * 4 + lax.axis_index("x")
    own_ref[...] = pltpu.roll(loss_ref[pl.ds(place // 4, 1), :], LANES - lax.rem(place, 4) * 32, 1)
    factor = 1.0 / (student_temp * ROWS * BATCHES)
    column_of_row(factor / total, prob_ref)
    column_of_row(factor * row_scale, target_ref)
    blocks = [pl.multiple_of(block_rows(p) * 32, 32) for p in range(8)]
    for j in range(COLS // CHUNK):
        cols = pl.ds(j * CHUNK, CHUNK)
        pieces = []
        for t in range(2):
            part = pl.ds(j * CHUNK + t * LANES, LANES)
            scale = column_ref[2 * j + t : 2 * j + t + 1, :]
            pieces.append(
                (exp_ref[:, part] * prob_ref[...] - weights_ref[:, part] * scale * target_ref[...]).astype(bf16)
            )
        score_grad = jnp.concatenate(pieces, axis=1)
        grad = jnp.dot(unit_t_ref[...], score_grad, preferred_element_type=f32)
        inverse = inverse_ref[:, cols]
        directions = jnp.concatenate([proto_ref[pl.ds(b, 32), cols] for b in blocks], axis=0) * inverse
        radial = jnp.sum(directions * grad, axis=0, keepdims=True)
        full = (grad - directions * radial) * inverse
        for s in range(4):
            kept_ref[s, :, cols] = full[s * 32 : s * 32 + 32, :]
            sent_ref[s, :, cols] = full[128 + s * 32 : 160 + s * 32, :]


def pair_kernel(kept_ref, came_ref, own_ref, up_ref, down_ref, far_up_ref, far_down_ref):
    far_up_ref[...] = kept_ref[2, 0:16, :] + came_ref[2, 0:16, :]
    far_down_ref[...] = kept_ref[2, 16:32, :] + came_ref[2, 16:32, :]
    own_ref[...] = kept_ref[0] + came_ref[0]
    up_ref[...] = kept_ref[1] + came_ref[1]
    down_ref[...] = kept_ref[3] + came_ref[3]


def pass_kernel(up_ref, down_ref, from_below_ref, from_above_ref, up_out_ref, down_out_ref):
    up_out_ref[0:16, :] = up_ref[0:16, :] + from_below_ref[...]
    up_out_ref[16:32, :] = up_ref[16:32, :]
    down_out_ref[0:16, :] = down_ref[0:16, :]
    down_out_ref[16:32, :] = down_ref[16:32, :] + from_above_ref[...]


def sum_kernel(own_ref, below_ref, above_ref, out_ref):
    out_ref[...] = own_ref[...] + below_ref[...] + above_ref[...]


def call(kernel, outs, scratch, ops, flops=0, elements=ROWS * COLS, inside=()):
    def shape(out):
        dims, dtype, kept = out
        return pltpu.VMEM(dims, dtype) if kept else jax.ShapeDtypeStruct(dims, dtype)

    def run(*operands):
        placed = [
            pltpu.with_memory_space_constraint(x, pltpu.VMEM) if i in inside else x for i, x in enumerate(operands)
        ]
        return pl.pallas_call(
            kernel,
            out_shape=[shape(o) for o in outs],
            in_specs=[pl.BlockSpec(memory_space=pltpu.VMEM)] * ops,
            out_specs=[pl.BlockSpec(memory_space=pltpu.VMEM)] * len(outs),
            scratch_shapes=scratch,
            compiler_params=pltpu.CompilerParams(vmem_limit_bytes=12 * 2**20),
            cost_estimate=pl.CostEstimate(flops=flops, bytes_accessed=4 * elements, transcendentals=0),
        )(*placed)

    return run


def share(value, axes, count):
    return lax.all_to_all(value, axes, 0, 0, tiled=True)


def shift(value, step):
    return lax.ppermute(value, "y", [(i, (i + step) % 4) for i in range(4)])


def scatter_sum(kept, sent):
    came = lax.ppermute(sent, "core", [(0, 1), (1, 0)])
    whole, half = ((32, COLS), f32, True), ((16, COLS), f32, True)
    own, up, down, far_up, far_down = call(pair_kernel, [whole, whole, whole, half, half], [], 2, elements=8 * 32 * COLS)(
        kept, came
    )
    up, down = call(pass_kernel, [whole, whole], [], 4, elements=4 * 32 * COLS)(
        up, down, shift(far_up, 1), shift(far_down, -1)
    )
    (out,) = call(sum_kernel, [((32, COLS), f32, False)], [], 3, elements=3 * 32 * COLS)(
        own, shift(up, 1), shift(down, -1)
    )
    return out


def on_device(student_codes, teacher_codes, prototypes):
    own_rows = student_codes.shape[0]
    big = ROWS * COLS
    table, column = ((ROWS, COLS), f32, True), ((COL_TILES, LANES), f32, True)
    to_batch, to_proto = ((BATCHES, COL_TILES, LANES), f32, True), ((PROTOS, ROW_TILES, LANES), f32, True)
    (pay,) = call(copy_kernel, [((PROTOS, 64, WIDTH), bf16, True)], [], 2, elements=PROTOS * 32 * WIDTH)(
        teacher_codes, student_codes
    )
    weights, scores, grown, unit_t, total, inverse, pay = call(
        score_kernel,
        [table, table, table, ((WIDTH, ROWS), bf16, True), ((ROW_TILES, LANES), f32, True), ((1, COLS), f32, True), to_batch],
        [
            pltpu.VMEM((ROWS, WIDTH), bf16),
            pltpu.VMEM((ROWS, WIDTH), bf16),
            pltpu.VMEM((1, COLS), f32),
            pltpu.VMEM((ROWS, LANES), f32),
        ],
        2,
        flops=4 * big * WIDTH,
        elements=3 * big,
    )(share(pay, PROTO, PROTOS), prototypes)
    for iteration in range(ITERS - 1):
        (pay,) = call(row_kernel, [to_proto], [pltpu.VMEM((ROWS, LANES), f32)], 2, inside=(1,))(
            share(pay, BATCH, BATCHES), weights
        )
        (pay,) = call(
            column_kernel,
            [to_batch],
            [pltpu.VMEM((ROWS, LANES), f32), pltpu.VMEM((COL_TILES, LANES), f32)],
            2,
            inside=(1,),
        )(share(pay, PROTO, PROTOS), weights)
    pay, column_scale = call(
        last_row_kernel,
        [((PROTOS, 3 * ROW_TILES, LANES), f32, True), column],
        [pltpu.VMEM((ROWS, LANES), f32), pltpu.VMEM((ROWS, LANES), f32), pltpu.VMEM((3 * ROW_TILES, LANES), f32)],
        4,
        elements=2 * big,
        inside=(1, 2, 3),
    )(share(pay, BATCH, BATCHES), weights, scores, total)
    kept, sent, own = call(
        grad_kernel,
        [((4, 32, COLS), f32, True), ((4, 32, COLS), f32, True), ((1, LANES), f32, False)],
        [pltpu.VMEM((ROWS, LANES), f32), pltpu.VMEM((ROWS, LANES), f32), pltpu.VMEM((ROW_TILES, LANES), f32)],
        7,
        flops=2 * big * WIDTH,
        elements=2 * big,
        inside=(1, 2, 3, 4, 6),
    )(share(pay, PROTO, PROTOS), weights, grown, column_scale, unit_t, prototypes, inverse)
    return (scatter_sum(kept, sent), own[0, :own_rows])


def solution(mesh):
    fine = Mesh(mesh.devices.reshape(4, 2, 8, 4), BATCH + PROTO)
    rows = P(BATCH + PROTO, None)
    return jax.shard_map(
        on_device,
        mesh=fine,
        in_specs=(rows, rows, P(None, PROTO)),
        out_specs=(P(BATCH, PROTO), P(BATCH + PROTO)),
        check_vma=False,
    )
```

```python
import functools

import jax
import jax.numpy as jnp
from jax import lax
from jax.experimental import pallas as pl
from jax.experimental.pallas import tpu as pltpu
from jax.sharding import Mesh, PartitionSpec as P

ITERS = 3

student_temp = 0.1
teacher_temp = 0.07
norm_eps = 1e-06

BATCH = ("y", "core")
PROTO = ("z", "x")
BATCHES = 8
PROTOS = 32
ROWS = 1024
COLS = 2048
WIDTH = 256
LANES = 128
ROW_TILES = ROWS // LANES
COL_TILES = COLS // LANES
CHUNK = 256
f32 = jnp.float32
bf16 = jnp.bfloat16


def unit_rows(values):
    values = values.astype(f32)
    return values * lax.rsqrt(jnp.sum(values * values, axis=-1, keepdims=True) + norm_eps)


def row_of_lane_sums(parts_ref, out_row, pieces=ROW_TILES):
    for g in range(pieces):
        block = parts_ref[pl.ds(g * LANES, LANES), :]
        out_row(g, jnp.sum(block.T, axis=0, keepdims=True))


def column_of_row(row, out_ref):
    for g in range(ROW_TILES):
        out_ref[pl.ds(g * LANES, LANES), :] = jnp.broadcast_to(row[g : g + 1, :], (LANES, LANES)).T


def spread_columns(column_mass, pay_ref):
    row = jnp.concatenate([column_mass[:, t * LANES : (t + 1) * LANES] for t in range(COL_TILES)], axis=0)
    for k in range(BATCHES):
        pay_ref[k] = row


def block_place(q):
    step = lax.rem(q // 2 - lax.axis_index("y") + 4, 4)
    return jnp.where(lax.axis_index("core") == q % 2, 0, 4) + step


def block_rows(p):
    row = lax.rem(lax.axis_index("y") + p % 4, 4)
    core = lax.axis_index("core")
    return 2 * row + (core if p < 4 else 1 - core)


def copy_kernel(teacher_hbm, student_hbm, pay_ref, student_ref, teacher_ref, sems):
    copies = [
        pltpu.make_async_copy(teacher_hbm, teacher_ref, sems.at[0]),
        pltpu.make_async_copy(student_hbm, student_ref, sems.at[1]),
    ]
    for copy in copies:
        copy.start()
    copies[0].wait()
    teacher = teacher_ref[...]
    for k in range(PROTOS):
        pay_ref[k] = teacher
    copies[1].wait()


def score_kernel(codes_ref, proto_hbm, weights_ref, low_ref, proto_ref, inverse_ref, pay_ref, unit_ref, mass_ref, sems):
    def chunk_copy(j):
        cols = pl.ds(pl.multiple_of(j * CHUNK, CHUNK), CHUNK)
        return pltpu.make_async_copy(proto_hbm.at[:, cols], proto_ref.at[:, cols], sems.at[j])

    for j in range(COLS // CHUNK):
        chunk_copy(j).start()
    for i in range(0, PROTOS, 4):
        unit_ref[pl.ds(i * 32, LANES), :] = unit_rows(codes_ref[i : i + 4].reshape(LANES, WIDTH)).astype(bf16)

    @pl.loop(0, COLS // CHUNK)
    def _(j):
        chunk_copy(j).wait()
        cols = pl.ds(pl.multiple_of(j * CHUNK, CHUNK), CHUNK)
        piece = proto_ref[:, cols]
        inverse = lax.rsqrt(jnp.sum(piece * piece, axis=0, keepdims=True) + norm_eps)
        inverse_ref[:, cols] = inverse
        low = (piece * inverse).astype(bf16)
        low_ref[:, cols] = low
        mass = jnp.zeros((8, CHUNK), f32)
        for i in range(0, ROWS, 256):
            rows = pl.ds(i, 256)
            scores = jnp.dot(unit_ref[rows, :], low, preferred_element_type=f32)
            weights = jnp.exp(scores * (1.0 / teacher_temp))
            weights_ref[rows, cols] = weights
            mass = mass + jnp.sum(weights.reshape(32, 8, CHUNK), axis=0)
        mass_ref[:, cols] = jnp.sum(mass, axis=0, keepdims=True)

    spread_columns(mass_ref[...], pay_ref)


def row_kernel(half, mass_ref, weights_ref, student_ref, pay_ref, parts_ref, row_ref):
    column = 1.0 / jnp.sum(mass_ref[...], axis=0)
    scale = [jnp.broadcast_to(column[t : t + 1, :], (8, LANES)) for t in range(COL_TILES)]

    @pl.loop(0, ROWS // 32)
    def _(i):
        for k in range(4):
            rows = pl.ds(pl.multiple_of(i * 32 + k * 8, 8), 8)
            mass = weights_ref[rows, pl.ds(0, LANES)] * scale[0]
            for t in range(1, COL_TILES):
                mass = mass + weights_ref[rows, pl.ds(t * LANES, LANES)] * scale[t]
            parts_ref[rows, :] = mass

    def put(g, row):
        row_ref[g : g + 1, :] = row

    row_of_lane_sums(parts_ref, put)
    high = row_ref[...].astype(bf16).astype(f32)
    row = jnp.concatenate([high, row_ref[...] - high], axis=0).astype(bf16)
    codes = [student_ref[pl.ds(half * 16, 16), pl.ds(t * LANES, LANES)] for t in range(2)]
    for k in range(PROTOS):
        pay_ref[k, 0:16, :] = row
        pay_ref[k, 16:32, :] = codes[0]
        pay_ref[k, 32:48, :] = codes[1]


def fold_lanes(value):
    return functools.reduce(lambda a, b: a + b, [value[:, t : t + LANES] for t in range(0, value.shape[1], LANES)])


def last_row_kernel(
    mass_ref,
    weights_ref,
    low_ref,
    first_ref,
    second_ref,
    pay_ref,
    column_ref,
    exp_ref,
    unit_t_ref,
    student_ref,
    mass_parts,
    total_parts,
    cross_parts,
    row_ref,
):
    column = 1.0 / jnp.sum(mass_ref[...], axis=0)
    column_ref[...] = column
    scale = jnp.concatenate([column[t : t + 1, :] for t in range(COL_TILES)], axis=1)
    place = [pl.multiple_of(block_place(q) * 32, 32) for q in range(8)]
    for part in (mass_parts, total_parts, cross_parts):
        part[...] = jnp.zeros_like(part)
    for i in range(0, PROTOS, 4):
        rows = pl.ds(i * 32, LANES)
        halves = [
            jnp.concatenate([ref[i : i + 4, 16:32, :], ref[i : i + 4, 32:48, :]], axis=2) for ref in (first_ref, second_ref)
        ]
        unit = unit_rows(jnp.concatenate(halves, axis=1).reshape(LANES, WIDTH))
        student_ref[rows, :] = unit.astype(bf16)
        turned = unit.T.astype(bf16)
        for q in range(8):
            unit_t_ref[pl.ds(place[q], 32), rows] = turned[q * 32 : q * 32 + 32, :]
    for j in range(0, COLS, 512):
        cols = pl.ds(j, 512)
        low = low_ref[:, cols]
        for i in range(0, ROWS, 256):
            rows = pl.ds(i, 256)
            scores = jnp.dot(student_ref[rows, :], low, preferred_element_type=f32)
            grown = jnp.exp(scores * (1.0 / student_temp))
            exp_ref[rows, cols] = grown
            total_parts[rows, :] += fold_lanes(grown)
            term = weights_ref[rows, cols] * scale[:, j : j + 512]
            mass_parts[rows, :] += fold_lanes(term)
            cross_parts[rows, :] += fold_lanes(term * scores)

    for k, part in enumerate((mass_parts, total_parts, cross_parts)):

        def put(g, row, k=k):
            row_ref[8 * k + g : 8 * k + g + 1, :] = row

        row_of_lane_sums(part, put)
    row = row_ref[...]
    for k in range(PROTOS):
        pay_ref[k] = row


def column_kernel(mass_ref, weights_ref, pay_ref, scale_ref, sums_ref):
    sums = jnp.sum(mass_ref[:, 0:16, :].astype(f32), axis=0)
    column_of_row(1.0 / (sums[0:8, :] + sums[8:16, :]), scale_ref)

    def step(i, sums):
        sums = list(sums)
        for k in range(2):
            rows = pl.ds(pl.multiple_of(i * 16 + k * 8, 8), 8)
            scale = scale_ref[rows, :]
            for t in range(COL_TILES):
                sums[t] = sums[t] + weights_ref[rows, pl.ds(t * LANES, LANES)] * scale
        return tuple(sums)

    sums = lax.fori_loop(0, ROWS // 16, step, tuple(jnp.zeros((8, LANES), f32) for _ in range(COL_TILES)))
    for t in range(COL_TILES):
        sums_ref[t : t + 1, :] = jnp.sum(sums[t], axis=0, keepdims=True)
    row = sums_ref[...]
    for k in range(BATCHES):
        pay_ref[k] = row


def grad_kernel(
    mass_ref,
    weights_ref,
    exp_ref,
    column_ref,
    unit_t_ref,
    proto_ref,
    inverse_ref,
    kept_ref,
    sent_ref,
    own_ref,
    prob_ref,
    target_ref,
    loss_ref,
):
    sums = jnp.sum(mass_ref[...], axis=0)
    row_scale = 1.0 / sums[0:8, :]
    total = sums[8:16, :]
    loss_ref[...] = jnp.log(total) - sums[16:24, :] * row_scale * (1.0 / student_temp)
    place = lax.axis_index("z") * 4 + lax.axis_index("x")
    own_ref[...] = pltpu.roll(loss_ref[pl.ds(place // 4, 1), :], LANES - lax.rem(place, 4) * 32, 1)
    factor = 1.0 / (student_temp * ROWS * BATCHES)
    column_of_row(factor / total, prob_ref)
    column_of_row(factor * row_scale, target_ref)
    blocks = [pl.multiple_of(block_rows(p) * 32, 32) for p in range(8)]
    for j in range(COLS // CHUNK):
        cols = pl.ds(j * CHUNK, CHUNK)
        pieces = []
        for t in range(2):
            part = pl.ds(j * CHUNK + t * LANES, LANES)
            scale = column_ref[2 * j + t : 2 * j + t + 1, :]
            pieces.append(
                (exp_ref[:, part] * prob_ref[...] - weights_ref[:, part] * scale * target_ref[...]).astype(bf16)
            )
        score_grad = jnp.concatenate(pieces, axis=1)
        grad = jnp.dot(unit_t_ref[...], score_grad, preferred_element_type=f32)
        inverse = inverse_ref[:, cols]
        directions = jnp.concatenate([proto_ref[pl.ds(b, 32), cols] for b in blocks], axis=0) * inverse
        radial = jnp.sum(directions * grad, axis=0, keepdims=True)
        full = (grad - directions * radial) * inverse
        for s in range(4):
            kept_ref[s, :, cols] = full[s * 32 : s * 32 + 32, :]
            sent_ref[s, :, cols] = full[128 + s * 32 : 160 + s * 32, :]


def pair_kernel(kept_ref, came_ref, own_ref, up_ref, down_ref, far_up_ref, far_down_ref):
    far_up_ref[...] = kept_ref[2, 0:16, :] + came_ref[2, 0:16, :]
    far_down_ref[...] = kept_ref[2, 16:32, :] + came_ref[2, 16:32, :]
    own_ref[...] = kept_ref[0] + came_ref[0]
    up_ref[...] = kept_ref[1] + came_ref[1]
    down_ref[...] = kept_ref[3] + came_ref[3]


def pass_kernel(up_ref, down_ref, from_below_ref, from_above_ref, up_out_ref, down_out_ref):
    up_out_ref[0:16, :] = up_ref[0:16, :] + from_below_ref[...]
    up_out_ref[16:32, :] = up_ref[16:32, :]
    down_out_ref[0:16, :] = down_ref[0:16, :]
    down_out_ref[16:32, :] = down_ref[16:32, :] + from_above_ref[...]


def sum_kernel(own_ref, below_ref, above_ref, out_ref):
    out_ref[...] = own_ref[...] + below_ref[...] + above_ref[...]


def call(kernel, outs, scratch, homes):
    spaces = {"v": pltpu.VMEM, "h": pltpu.HBM}

    def shape(out):
        dims, dtype, kept = out
        return pltpu.VMEM(dims, dtype) if kept else jax.ShapeDtypeStruct(dims, dtype)

    def run(*operands):
        placed = [
            pltpu.with_memory_space_constraint(x, spaces[h]) if h in spaces else x for x, h in zip(operands, homes)
        ]
        return pl.pallas_call(
            kernel,
            out_shape=[shape(o) for o in outs],
            in_specs=[pl.BlockSpec(memory_space=pl.ANY if h == "h" else pltpu.VMEM) for h in homes],
            out_specs=[pl.BlockSpec(memory_space=pltpu.VMEM if o[2] is not None else pl.ANY) for o in outs],
            scratch_shapes=scratch,
            compiler_params=pltpu.CompilerParams(vmem_limit_bytes=12 * 2**20),
            cost_estimate=pl.CostEstimate(flops=0, bytes_accessed=0, transcendentals=0),
        )(*placed)

    return run


def share(value, axes, count):
    return lax.all_to_all(value, axes, 0, 0, tiled=True)


def shift(value, step):
    return lax.ppermute(value, "y", [(i, (i + step) % 4) for i in range(4)])


def scatter_sum(kept, sent):
    came = lax.ppermute(sent, "core", [(0, 1), (1, 0)])
    whole, half = ((32, COLS), f32, True), ((16, COLS), f32, True)
    own, up, down, far_up, far_down = call(pair_kernel, [whole, whole, whole, half, half], [], "vv")(kept, came)
    up, down = call(pass_kernel, [whole, whole], [], "vvvv")(up, down, shift(far_up, 1), shift(far_down, -1))
    (out,) = call(sum_kernel, [((32, COLS), f32, False)], [], "vvv")(own, shift(up, 1), shift(down, -1))
    return out


def on_device(student_codes, teacher_codes, prototypes):
    own_rows = student_codes.shape[0]
    table, column = ((ROWS, COLS), f32, True), ((COL_TILES, LANES), f32, True)
    to_batch, to_proto = ((BATCHES, COL_TILES, LANES), f32, True), ((PROTOS, 48, LANES), bf16, True)
    lanes, units, row = pltpu.VMEM((ROWS, LANES), f32), pltpu.VMEM((ROWS, WIDTH), bf16), pltpu.VMEM((ROW_TILES, LANES), f32)
    pay, student = call(
        copy_kernel,
        [((PROTOS, own_rows, WIDTH), bf16, True), ((own_rows, WIDTH), bf16, True)],
        [pltpu.VMEM((own_rows, WIDTH), bf16), pltpu.SemaphoreType.DMA((2,))],
        "hh",
    )(teacher_codes, student_codes)
    weights, low, protos, inverse, pay = call(
        score_kernel,
        [table, ((WIDTH, COLS), bf16, True), ((WIDTH, COLS), f32, True), ((1, COLS), f32, True), to_batch],
        [units, pltpu.VMEM((1, COLS), f32), pltpu.SemaphoreType.DMA((COLS // CHUNK,))],
        "vh",
    )(share(pay, PROTO, PROTOS), prototypes)
    came = []
    for half in range(ITERS - 1):
        (pay,) = call(functools.partial(row_kernel, half), [to_proto], [lanes, row], "vvv")(
            share(pay, BATCH, BATCHES), weights, student
        )
        came.append(share(pay, PROTO, PROTOS))
        (pay,) = call(column_kernel, [to_batch], [lanes, pltpu.VMEM((COL_TILES, LANES), f32)], "vv")(came[-1], weights)
    pay, column_scale, grown, unit_t = call(
        last_row_kernel,
        [((PROTOS, 3 * ROW_TILES, LANES), f32, True), column, table, ((WIDTH, ROWS), bf16, True)],
        [units, lanes, lanes, lanes, pltpu.VMEM((3 * ROW_TILES, LANES), f32)],
        "vvvvv",
    )(share(pay, BATCH, BATCHES), weights, low, *came)
    kept, sent, own = call(
        grad_kernel,
        [((4, 32, COLS), f32, True), ((4, 32, COLS), f32, True), ((1, LANES), f32, False)],
        [lanes, lanes, row],
        "vvvvvvv",
    )(share(pay, PROTO, PROTOS), weights, grown, column_scale, unit_t, protos, inverse)
    return (scatter_sum(kept, sent), own[0, :own_rows])


def solution(mesh):
    fine = Mesh(mesh.devices.reshape(4, 2, 8, 4), BATCH + PROTO)
    rows = P(BATCH + PROTO, None)
    return jax.shard_map(
        on_device,
        mesh=fine,
        in_specs=(rows, rows, P(None, PROTO)),
        out_specs=(P(BATCH, PROTO), P(BATCH + PROTO)),
        check_vma=False,
    )
```

```python
import functools

import jax
import jax.numpy as jnp
from jax import lax
from jax.experimental import pallas as pl
from jax.experimental.pallas import tpu as pltpu
from jax.sharding import Mesh, PartitionSpec as P

ITERS = 3

student_temp = 0.1
teacher_temp = 0.07
norm_eps = 1e-06
log2_e = 1.4426950408889634

BATCH = ("y", "core")
PROTO = ("z", "x")
BATCHES = 8
PROTOS = 32
ROWS = 1024
COLS = 2048
WIDTH = 256
LANES = 128
ROW_TILES = ROWS // LANES
COL_TILES = COLS // LANES
CHUNK = 256
FLAT = ROWS + LANES
OWN = ROWS // PROTOS
f32 = jnp.float32
bf16 = jnp.bfloat16


def unit_rows(values):
    values = values.astype(f32)
    return values * lax.rsqrt(jnp.sum(values * values, axis=-1, keepdims=True) + norm_eps)


def row_of_lane_sums(parts_ref, out_row, pieces=ROW_TILES):
    for g in range(pieces):
        block = parts_ref[pl.ds(g * LANES, LANES), :]
        out_row(g, jnp.sum(block.T, axis=0, keepdims=True))


def column_of_row(row, out_ref):
    for g in range(ROW_TILES):
        out_ref[pl.ds(g * LANES, LANES), :] = jnp.broadcast_to(row[g : g + 1, :], (LANES, LANES)).T


def spread_columns(column_mass, pay_ref):
    row = jnp.concatenate([column_mass[:, t * LANES : (t + 1) * LANES] for t in range(COL_TILES)], axis=0)
    for k in range(BATCHES):
        pay_ref[k] = row


def block_place(q):
    step = lax.rem(q // 2 - lax.axis_index("y") + 4, 4)
    return jnp.where(lax.axis_index("core") == q % 2, 0, 4) + step


def block_rows(p):
    row = lax.rem(lax.axis_index("y") + p % 4, 4)
    core = lax.axis_index("core")
    return 2 * row + (core if p < 4 else 1 - core)


def owned_piece(row, k):
    return pltpu.roll(row[k // 4 : k // 4 + 1, :], (LANES - (k % 4) * OWN) % LANES, 1)


def flat_row(row):
    return jnp.concatenate([row[g : g + 1, :] for g in range(ROW_TILES)], axis=1)


def flat_rows(flat):
    return jnp.concatenate([flat[:, g * LANES : (g + 1) * LANES] for g in range(ROW_TILES)], axis=0)


def copy_kernel(teacher_hbm, student_hbm, proto_hbm, pay_ref, proto_ref, codes_ref, sems):
    copies = [
        pltpu.make_async_copy(teacher_hbm, codes_ref.at[0], sems.at[0]),
        pltpu.make_async_copy(student_hbm, codes_ref.at[1], sems.at[1]),
        pltpu.make_async_copy(proto_hbm, proto_ref, sems.at[2]),
    ]
    for copy in copies:
        copy.start()
    copies[0].wait()
    copies[1].wait()
    for t in range(2):
        codes = codes_ref[t]
        for k in range(PROTOS):
            pay_ref[k, pl.ds(t * OWN, OWN), :] = codes
    copies[2].wait()


def score_kernel(
    codes_ref,
    proto_ref,
    weights_ref,
    scores_ref,
    exp_ref,
    unit_t_ref,
    total_ref,
    inverse_ref,
    pay_ref,
    teacher_ref,
    student_ref,
    mass_ref,
    parts_ref,
):
    place = [pl.multiple_of(block_place(q) * 32, 32) for q in range(8)]
    for i in range(0, PROTOS, 4):
        rows = pl.ds(i * OWN, LANES)
        teacher_ref[rows, :] = unit_rows(codes_ref[i : i + 4, 0:OWN, :].reshape(LANES, WIDTH)).astype(bf16)
        unit = unit_rows(codes_ref[i : i + 4, OWN : 2 * OWN, :].reshape(LANES, WIDTH))
        student_ref[rows, :] = unit.astype(bf16)
        turned = unit.T.astype(bf16)
        for q in range(8):
            unit_t_ref[pl.ds(place[q], 32), rows] = turned[q * 32 : q * 32 + 32, :]
    parts_ref[...] = jnp.zeros_like(parts_ref)

    @pl.loop(0, COLS // CHUNK)
    def _(j):
        cols = pl.ds(pl.multiple_of(j * CHUNK, CHUNK), CHUNK)
        piece = proto_ref[:, cols]
        inverse = lax.rsqrt(jnp.sum(piece * piece, axis=0, keepdims=True) + norm_eps)
        inverse_ref[:, cols] = inverse
        low = (piece * inverse).astype(bf16)
        mass = jnp.zeros((8, CHUNK), f32)
        for i in range(0, ROWS, 256):
            rows = pl.ds(i, 256)
            scores = jnp.dot(teacher_ref[rows, :], low, preferred_element_type=f32)
            weights = jnp.exp2(scores * (log2_e / teacher_temp))
            weights_ref[rows, cols] = weights
            mass = mass + jnp.sum(weights.reshape(32, 8, CHUNK), axis=0)
        mass_ref[:, cols] = jnp.sum(mass, axis=0, keepdims=True)
        for i in range(0, ROWS, 256):
            rows = pl.ds(i, 256)
            scores = jnp.dot(student_ref[rows, :], low, preferred_element_type=f32)
            scores_ref[rows, cols] = scores
            grown = jnp.exp2(scores * (log2_e / student_temp))
            exp_ref[rows, cols] = grown
            parts_ref[rows, :] += grown[:, :LANES] + grown[:, LANES:]

    spread_columns(mass_ref[...], pay_ref)

    def put(g, row):
        total_ref[g : g + 1, :] = row

    row_of_lane_sums(parts_ref, put)


def scaled_rows(column, weights_ref, parts_ref, scores_ref=None, cross_ref=None):
    scale = [jnp.broadcast_to(column[t : t + 1, :], (8, LANES)) for t in range(COL_TILES)]

    @pl.loop(0, ROWS // 32)
    def _(i):
        for k in range(4):
            rows = pl.ds(pl.multiple_of(i * 32 + k * 8, 8), 8)
            mass = cross = None
            for t in range(COL_TILES):
                cols = pl.ds(t * LANES, LANES)
                term = weights_ref[rows, cols] * scale[t]
                mass = term if mass is None else mass + term
                if scores_ref is not None:
                    term = term * scores_ref[rows, cols]
                    cross = term if cross is None else cross + term
            parts_ref[rows, :] = mass
            if scores_ref is not None:
                cross_ref[rows, :] = cross


def row_kernel(spread, mass_ref, weights_ref, extra_ref, pay_ref, parts_ref, row_ref):
    scaled_rows(1.0 / jnp.sum(mass_ref[...], axis=0), weights_ref, parts_ref)

    def put(g, row):
        row_ref[g : g + 1, :] = row

    row_of_lane_sums(parts_ref, put)
    flat, extra = flat_row(row_ref[...]), extra_ref[...]
    for k in range(PROTOS):
        pay_ref[k, :, 0:ROWS] = flat
        pay_ref[k, :, ROWS:FLAT] = owned_piece(extra, k) if spread else extra


def last_row_kernel(mass_ref, weights_ref, scores_ref, pay_ref, column_ref, parts_ref, cross_ref, row_ref):
    column = 1.0 / jnp.sum(mass_ref[...], axis=0)
    column_ref[...] = column
    scaled_rows(column, weights_ref, parts_ref, scores_ref, cross_ref)

    def put_mass(g, row):
        row_ref[g : g + 1, :] = row

    def put_cross(g, row):
        row_ref[ROW_TILES + g : ROW_TILES + g + 1, :] = row

    row_of_lane_sums(parts_ref, put_mass)
    row_of_lane_sums(cross_ref, put_cross)
    flat, cross = flat_row(row_ref[0:ROW_TILES, :]), row_ref[ROW_TILES : 2 * ROW_TILES, :]
    for k in range(PROTOS):
        pay_ref[k, :, 0:ROWS] = flat
        pay_ref[k, :, ROWS:FLAT] = owned_piece(cross, k)


def column_kernel(gather, mass_ref, weights_ref, pay_ref, extra_ref, scale_ref, sums_ref):
    sums = jnp.sum(mass_ref[...], axis=0)
    column_of_row(1.0 / flat_rows(sums), scale_ref)
    if gather:
        lane = lax.broadcasted_iota(jnp.int32, (1, LANES), 1)
        for g in range(ROW_TILES):
            row = jnp.zeros((1, LANES), f32)
            for t in range(4):
                piece = jnp.where(lane < OWN, mass_ref[4 * g + t, :, ROWS:FLAT], 0.0)
                row = row + (pltpu.roll(piece, t * OWN, 1) if t else piece)
            extra_ref[g : g + 1, :] = row
    else:
        extra_ref[...] = sums[:, ROWS:FLAT]

    def step(i, sums):
        sums = list(sums)
        for k in range(2):
            rows = pl.ds(pl.multiple_of(i * 16 + k * 8, 8), 8)
            scale = scale_ref[rows, :]
            for t in range(COL_TILES):
                sums[t] = sums[t] + weights_ref[rows, pl.ds(t * LANES, LANES)] * scale
        return tuple(sums)

    sums = lax.fori_loop(0, ROWS // 16, step, tuple(jnp.zeros((8, LANES), f32) for _ in range(COL_TILES)))
    for t in range(COL_TILES):
        sums_ref[t : t + 1, :] = jnp.sum(sums[t], axis=0, keepdims=True)
    row = sums_ref[...]
    for k in range(BATCHES):
        pay_ref[k] = row


def grad_kernel(
    mass_ref,
    weights_ref,
    exp_ref,
    column_ref,
    total_ref,
    unit_t_ref,
    proto_ref,
    inverse_ref,
    kept_ref,
    sent_ref,
    own_ref,
    prob_ref,
    target_ref,
    row_ref,
):
    sums = jnp.sum(mass_ref[...], axis=0)
    row_ref[...] = 1.0 / flat_rows(sums)
    factor = 1.0 / (student_temp * ROWS * BATCHES)
    column_of_row(factor / total_ref[...], prob_ref)
    column_of_row(factor * row_ref[...], target_ref)
    place = lax.axis_index("z") * 4 + lax.axis_index("x")
    line, turn = pl.ds(place // 4, 1), LANES - lax.rem(place, 4) * OWN
    row_scale = pltpu.roll(row_ref[line, :], turn, 1)
    total = pltpu.roll(total_ref[line, :], turn, 1)
    own_ref[...] = jnp.log(total) - sums[:, ROWS:FLAT] * row_scale * (1.0 / student_temp)
    blocks = [pl.multiple_of(block_rows(p) * 32, 32) for p in range(8)]
    for j in range(COLS // CHUNK):
        cols = pl.ds(j * CHUNK, CHUNK)
        pieces = []
        for t in range(2):
            part = pl.ds(j * CHUNK + t * LANES, LANES)
            scale = column_ref[2 * j + t : 2 * j + t + 1, :]
            pieces.append(
                (exp_ref[:, part] * prob_ref[...] - weights_ref[:, part] * scale * target_ref[...]).astype(bf16)
            )
        score_grad = jnp.concatenate(pieces, axis=1)
        grad = jnp.dot(unit_t_ref[...], score_grad, preferred_element_type=f32)
        inverse = inverse_ref[:, cols]
        directions = jnp.concatenate([proto_ref[pl.ds(b, 32), cols] for b in blocks], axis=0) * inverse
        radial = jnp.sum(directions * grad, axis=0, keepdims=True)
        full = (grad - directions * radial) * inverse
        for s in range(4):
            kept_ref[s, :, cols] = full[s * 32 : s * 32 + 32, :]
            sent_ref[s, :, cols] = full[128 + s * 32 : 160 + s * 32, :]


def pair_kernel(kept_ref, came_ref, own_ref, up_ref, down_ref, far_up_ref, far_down_ref):
    far_up_ref[...] = kept_ref[2, 0:16, :] + came_ref[2, 0:16, :]
    far_down_ref[...] = kept_ref[2, 16:32, :] + came_ref[2, 16:32, :]
    own_ref[...] = kept_ref[0] + came_ref[0]
    up_ref[...] = kept_ref[1] + came_ref[1]
    down_ref[...] = kept_ref[3] + came_ref[3]


def pass_kernel(up_ref, down_ref, from_below_ref, from_above_ref, up_out_ref, down_out_ref):
    up_out_ref[0:16, :] = up_ref[0:16, :] + from_below_ref[...]
    up_out_ref[16:32, :] = up_ref[16:32, :]
    down_out_ref[0:16, :] = down_ref[0:16, :]
    down_out_ref[16:32, :] = down_ref[16:32, :] + from_above_ref[...]


def sum_kernel(own_ref, below_ref, above_ref, out_ref):
    out_ref[...] = own_ref[...] + below_ref[...] + above_ref[...]


def call(kernel, outs, scratch, homes):
    spaces = {"v": pltpu.VMEM, "h": pltpu.HBM}

    def shape(out):
        dims, dtype, kept = out
        return pltpu.VMEM(dims, dtype) if kept else jax.ShapeDtypeStruct(dims, dtype)

    def run(*operands):
        placed = [
            pltpu.with_memory_space_constraint(x, spaces[h]) if h in spaces else x for x, h in zip(operands, homes)
        ]
        return pl.pallas_call(
            kernel,
            out_shape=[shape(o) for o in outs],
            in_specs=[pl.BlockSpec(memory_space=pl.ANY if h == "h" else pltpu.VMEM) for h in homes],
            out_specs=[pl.BlockSpec(memory_space=pltpu.VMEM if o[2] is not None else pl.ANY) for o in outs],
            scratch_shapes=scratch,
            compiler_params=pltpu.CompilerParams(vmem_limit_bytes=12 * 2**20),
            cost_estimate=pl.CostEstimate(flops=0, bytes_accessed=0, transcendentals=0),
        )(*placed)

    return run


def share(value, axes, count):
    return lax.all_to_all(value, axes, 0, 0, tiled=True)


def shift(value, step):
    return lax.ppermute(value, "y", [(i, (i + step) % 4) for i in range(4)])


def scatter_sum(kept, sent):
    came = lax.ppermute(sent, "core", [(0, 1), (1, 0)])
    whole, half = ((32, COLS), f32, True), ((16, COLS), f32, True)
    own, up, down, far_up, far_down = call(pair_kernel, [whole, whole, whole, half, half], [], "vv")(kept, came)
    up, down = call(pass_kernel, [whole, whole], [], "vvvv")(up, down, shift(far_up, 1), shift(far_down, -1))
    (out,) = call(sum_kernel, [((32, COLS), f32, False)], [], "vvv")(own, shift(up, 1), shift(down, -1))
    return out


def on_device(student_codes, teacher_codes, prototypes):
    table, column = ((ROWS, COLS), f32, True), ((COL_TILES, LANES), f32, True)
    to_batch, to_proto = ((BATCHES, COL_TILES, LANES), f32, True), ((PROTOS, 1, FLAT), f32, True)
    crops, owned = ((ROW_TILES, LANES), f32, True), ((1, LANES), f32, True)
    lanes, units, row = pltpu.VMEM((ROWS, LANES), f32), pltpu.VMEM((ROWS, WIDTH), bf16), pltpu.VMEM((ROW_TILES, LANES), f32)
    pay, protos = call(
        copy_kernel,
        [((PROTOS, 2 * OWN, WIDTH), bf16, True), ((WIDTH, COLS), f32, True)],
        [pltpu.VMEM((2, OWN, WIDTH), bf16), pltpu.SemaphoreType.DMA((3,))],
        "hhh",
    )(teacher_codes, student_codes, prototypes)
    weights, scores, grown, unit_t, extra, inverse, pay = call(
        score_kernel,
        [table, table, table, ((WIDTH, ROWS), bf16, True), crops, ((1, COLS), f32, True), to_batch],
        [units, units, pltpu.VMEM((1, COLS), f32), lanes],
        "vv",
    )(share(pay, PROTO, PROTOS), protos)
    for iteration in range(ITERS - 1):
        first = iteration == 0
        (pay,) = call(functools.partial(row_kernel, first), [to_proto], [lanes, row], "vvv")(
            share(pay, BATCH, BATCHES), weights, extra
        )
        pay, extra = call(
            functools.partial(column_kernel, not first),
            [to_batch, owned if first else crops],
            [lanes, pltpu.VMEM((COL_TILES, LANES), f32)],
            "vv",
        )(share(pay, PROTO, PROTOS), weights)
    pay, column_scale = call(
        last_row_kernel,
        [to_proto, column],
        [lanes, lanes, pltpu.VMEM((2 * ROW_TILES, LANES), f32)],
        "vvv",
    )(share(pay, BATCH, BATCHES), weights, scores)
    kept, sent, own = call(
        grad_kernel,
        [((4, 32, COLS), f32, True), ((4, 32, COLS), f32, True), ((1, LANES), f32, False)],
        [lanes, lanes, row],
        "vvvvvvvv",
    )(share(pay, PROTO, PROTOS), weights, grown, column_scale, extra, unit_t, protos, inverse)
    return (scatter_sum(kept, sent), own[0, :OWN])


def solution(mesh):
    fine = Mesh(mesh.devices.reshape(4, 2, 8, 4), BATCH + PROTO)
    rows = P(BATCH + PROTO, None)
    return jax.shard_map(
        on_device,
        mesh=fine,
        in_specs=(rows, rows, P(None, PROTO)),
        out_specs=(P(BATCH, PROTO), P(BATCH + PROTO)),
        check_vma=False,
    )
```

```python
import functools

import jax
import jax.numpy as jnp
from jax import lax
from jax.experimental import pallas as pl
from jax.experimental.pallas import tpu as pltpu
from jax.sharding import Mesh, PartitionSpec as P

ITERS = 3

student_temp = 0.1
teacher_temp = 0.07
norm_eps = 1e-06
log2_e = 1.4426950408889634

BATCH = ("y", "core")
PROTO = ("z", "x")
BATCHES = 8
PROTOS = 32
ROWS = 1024
COLS = 2048
WIDTH = 256
LANES = 128
ROW_TILES = ROWS // LANES
COL_TILES = COLS // LANES
CHUNK = 256
FLAT = ROWS + LANES
OWN = ROWS // PROTOS
ZS = 8
XS = 4
BLOCK = ROWS // XS
f32 = jnp.float32
bf16 = jnp.bfloat16


def unit_rows(values):
    values = values.astype(f32)
    return values * lax.rsqrt(jnp.sum(values * values, axis=-1, keepdims=True) + norm_eps)


def row_of_lane_sums(parts_ref, out_row, pieces=ROW_TILES):
    for g in range(pieces):
        block = parts_ref[pl.ds(g * LANES, LANES), :]
        out_row(g, jnp.sum(block.T, axis=0, keepdims=True))


def column_of_row(row, out_ref):
    for g in range(ROW_TILES):
        out_ref[pl.ds(g * LANES, LANES), :] = jnp.broadcast_to(row[g : g + 1, :], (LANES, LANES)).T


def spread_columns(column_mass, pay_ref):
    row = jnp.concatenate([column_mass[:, t * LANES : (t + 1) * LANES] for t in range(COL_TILES)], axis=0)
    for k in range(BATCHES):
        pay_ref[k] = row


def block_place(q):
    step = lax.rem(q // 2 - lax.axis_index("y") + 4, 4)
    return jnp.where(lax.axis_index("core") == q % 2, 0, 4) + step


def block_rows(p):
    row = lax.rem(lax.axis_index("y") + p % 4, 4)
    core = lax.axis_index("core")
    return 2 * row + (core if p < 4 else 1 - core)


def owned_piece(row, k):
    z, x = k // XS, k % XS
    line = 2 * x + z // 4
    return pltpu.roll(row[line : line + 1, :], (LANES - (z % 4) * OWN) % LANES, 1)


def flat_row(row):
    return jnp.concatenate([row[g : g + 1, :] for g in range(ROW_TILES)], axis=1)


def flat_rows(flat):
    return jnp.concatenate([flat[:, g * LANES : (g + 1) * LANES] for g in range(ROW_TILES)], axis=0)


def copy_kernel(teacher_hbm, student_hbm, proto_hbm, pay_ref, proto_ref, codes_ref, sems):
    copies = [
        pltpu.make_async_copy(teacher_hbm, codes_ref.at[0], sems.at[0]),
        pltpu.make_async_copy(student_hbm, codes_ref.at[1], sems.at[1]),
        pltpu.make_async_copy(proto_hbm, proto_ref, sems.at[2]),
    ]
    for copy in copies:
        copy.start()
    copies[0].wait()
    copies[1].wait()
    for t in range(2):
        unit = unit_rows(codes_ref[t]).astype(bf16)
        for k in range(ZS):
            pay_ref[k, pl.ds(t * OWN, OWN), :] = unit
    copies[2].wait()


def split_kernel(came_ref, teacher_ref, student_ref):
    teacher_ref[...] = came_ref[:, 0:OWN, :].reshape(BLOCK, WIDTH)
    student_ref[...] = came_ref[:, OWN : 2 * OWN, :].reshape(BLOCK, WIDTH)


def norm_kernel(proto_ref, after_ref, low_ref, inverse_ref):
    for j in range(0, COLS, CHUNK):
        cols = pl.ds(j, CHUNK)
        piece = proto_ref[:, cols]
        inverse = lax.rsqrt(jnp.sum(piece * piece, axis=0, keepdims=True) + norm_eps)
        inverse_ref[:, cols] = inverse
        low_ref[:, cols] = (piece * inverse).astype(bf16)


def block_starts():
    x = lax.axis_index("x")
    return [pl.multiple_of(lax.rem(x + XS - k, XS) * BLOCK, BLOCK) for k in range(XS)]


def teacher_kernel(u0_ref, u1_ref, u2_ref, u3_ref, low_ref, weights_ref, mass_ref):
    starts = block_starts()

    @pl.loop(0, COLS // CHUNK)
    def _(j):
        cols = pl.ds(pl.multiple_of(j * CHUNK, CHUNK), CHUNK)
        low = low_ref[:, cols]
        mass = jnp.zeros((8, CHUNK), f32)
        for unit_ref, start in zip((u0_ref, u1_ref, u2_ref, u3_ref), starts):
            scores = jnp.dot(unit_ref[...], low, preferred_element_type=f32)
            weights = jnp.exp2(scores * (log2_e / teacher_temp))
            weights_ref[pl.ds(start, BLOCK), cols] = weights
            mass = mass + jnp.sum(weights.reshape(BLOCK // 8, 8, CHUNK), axis=0)
        mass_ref[:, cols] = jnp.sum(mass, axis=0, keepdims=True)


def student_kernel(
    u0_ref, u1_ref, u2_ref, u3_ref, low_ref, mass_ref, scores_ref, exp_ref, unit_t_ref, total_ref, pay_ref, parts_ref
):
    starts = block_starts()
    place = [pl.multiple_of(block_place(q) * 32, 32) for q in range(8)]
    units = (u0_ref, u1_ref, u2_ref, u3_ref)
    for unit_ref, start in zip(units, starts):
        turned = unit_ref[...].astype(f32).T.astype(bf16)
        for q in range(8):
            unit_t_ref[pl.ds(place[q], 32), pl.ds(start, BLOCK)] = turned[q * 32 : q * 32 + 32, :]
    parts_ref[...] = jnp.zeros_like(parts_ref)

    @pl.loop(0, COLS // CHUNK)
    def _(j):
        cols = pl.ds(pl.multiple_of(j * CHUNK, CHUNK), CHUNK)
        low = low_ref[:, cols]
        for unit_ref, start in zip(units, starts):
            rows = pl.ds(start, BLOCK)
            scores = jnp.dot(unit_ref[...], low, preferred_element_type=f32)
            scores_ref[rows, cols] = scores
            grown = jnp.exp2(scores * (log2_e / student_temp))
            exp_ref[rows, cols] = grown
            parts_ref[rows, :] += grown[:, :LANES] + grown[:, LANES:]

    spread_columns(mass_ref[...], pay_ref)

    def put(g, row):
        total_ref[g : g + 1, :] = row

    row_of_lane_sums(parts_ref, put)


def scaled_rows(column, weights_ref, parts_ref, scores_ref=None, cross_ref=None):
    scale = [jnp.broadcast_to(column[t : t + 1, :], (8, LANES)) for t in range(COL_TILES)]

    @pl.loop(0, ROWS // 32)
    def _(i):
        for k in range(4):
            rows = pl.ds(pl.multiple_of(i * 32 + k * 8, 8), 8)
            mass = cross = None
            for t in range(COL_TILES):
                cols = pl.ds(t * LANES, LANES)
                term = weights_ref[rows, cols] * scale[t]
                mass = term if mass is None else mass + term
                if scores_ref is not None:
                    term = term * scores_ref[rows, cols]
                    cross = term if cross is None else cross + term
            parts_ref[rows, :] = mass
            if scores_ref is not None:
                cross_ref[rows, :] = cross


def row_kernel(spread, mass_ref, weights_ref, extra_ref, pay_ref, parts_ref, row_ref):
    scaled_rows(1.0 / jnp.sum(mass_ref[...], axis=0), weights_ref, parts_ref)

    def put(g, row):
        row_ref[g : g + 1, :] = row

    row_of_lane_sums(parts_ref, put)
    flat, extra = flat_row(row_ref[...]), extra_ref[...]
    for k in range(PROTOS):
        pay_ref[k, :, 0:ROWS] = flat
        pay_ref[k, :, ROWS:FLAT] = owned_piece(extra, k) if spread else extra


def last_row_kernel(mass_ref, weights_ref, scores_ref, pay_ref, column_ref, parts_ref, cross_ref, row_ref):
    column = 1.0 / jnp.sum(mass_ref[...], axis=0)
    column_ref[...] = column
    scaled_rows(column, weights_ref, parts_ref, scores_ref, cross_ref)

    def put_mass(g, row):
        row_ref[g : g + 1, :] = row

    def put_cross(g, row):
        row_ref[ROW_TILES + g : ROW_TILES + g + 1, :] = row

    row_of_lane_sums(parts_ref, put_mass)
    row_of_lane_sums(cross_ref, put_cross)
    flat, cross = flat_row(row_ref[0:ROW_TILES, :]), row_ref[ROW_TILES : 2 * ROW_TILES, :]
    for k in range(PROTOS):
        pay_ref[k, :, 0:ROWS] = flat
        pay_ref[k, :, ROWS:FLAT] = owned_piece(cross, k)


def column_kernel(gather, mass_ref, weights_ref, pay_ref, extra_ref, scale_ref, sums_ref):
    sums = jnp.sum(mass_ref[...], axis=0)
    column_of_row(1.0 / flat_rows(sums), scale_ref)
    if gather:
        lane = lax.broadcasted_iota(jnp.int32, (1, LANES), 1)
        for g in range(ROW_TILES):
            row = jnp.zeros((1, LANES), f32)
            for t in range(4):
                piece = jnp.where(lane < OWN, mass_ref[(4 * (g % 2) + t) * XS + g // 2, :, ROWS:FLAT], 0.0)
                row = row + (pltpu.roll(piece, t * OWN, 1) if t else piece)
            extra_ref[g : g + 1, :] = row
    else:
        extra_ref[...] = sums[:, ROWS:FLAT]

    def step(i, sums):
        sums = list(sums)
        for k in range(2):
            rows = pl.ds(pl.multiple_of(i * 16 + k * 8, 8), 8)
            scale = scale_ref[rows, :]
            for t in range(COL_TILES):
                sums[t] = sums[t] + weights_ref[rows, pl.ds(t * LANES, LANES)] * scale
        return tuple(sums)

    sums = lax.fori_loop(0, ROWS // 16, step, tuple(jnp.zeros((8, LANES), f32) for _ in range(COL_TILES)))
    for t in range(COL_TILES):
        sums_ref[t : t + 1, :] = jnp.sum(sums[t], axis=0, keepdims=True)
    row = sums_ref[...]
    for k in range(BATCHES):
        pay_ref[k] = row


def grad_kernel(
    mass_ref,
    weights_ref,
    exp_ref,
    column_ref,
    total_ref,
    unit_t_ref,
    proto_ref,
    inverse_ref,
    kept_ref,
    sent_ref,
    own_ref,
    prob_ref,
    target_ref,
    row_ref,
):
    sums = jnp.sum(mass_ref[...], axis=0)
    row_ref[...] = 1.0 / flat_rows(sums)
    factor = 1.0 / (student_temp * ROWS * BATCHES)
    column_of_row(factor / total_ref[...], prob_ref)
    column_of_row(factor * row_ref[...], target_ref)
    z = lax.axis_index("z")
    line, turn = pl.ds(2 * lax.axis_index("x") + z // 4, 1), LANES - lax.rem(z, 4) * OWN
    row_scale = pltpu.roll(row_ref[line, :], turn, 1)
    total = pltpu.roll(total_ref[line, :], turn, 1)
    own_ref[...] = jnp.log(total) - sums[:, ROWS:FLAT] * row_scale * (1.0 / student_temp)
    blocks = [pl.multiple_of(block_rows(p) * 32, 32) for p in range(8)]
    for j in range(COLS // CHUNK):
        cols = pl.ds(j * CHUNK, CHUNK)
        pieces = []
        for t in range(2):
            part = pl.ds(j * CHUNK + t * LANES, LANES)
            scale = column_ref[2 * j + t : 2 * j + t + 1, :]
            pieces.append(
                (exp_ref[:, part] * prob_ref[...] - weights_ref[:, part] * scale * target_ref[...]).astype(bf16)
            )
        score_grad = jnp.concatenate(pieces, axis=1)
        grad = jnp.dot(unit_t_ref[...], score_grad, preferred_element_type=f32)
        inverse = inverse_ref[:, cols]
        directions = jnp.concatenate([proto_ref[pl.ds(b, 32), cols] for b in blocks], axis=0) * inverse
        radial = jnp.sum(directions * grad, axis=0, keepdims=True)
        full = (grad - directions * radial) * inverse
        for s in range(4):
            kept_ref[s, :, cols] = full[s * 32 : s * 32 + 32, :]
            sent_ref[s, :, cols] = full[128 + s * 32 : 160 + s * 32, :]


def pair_kernel(kept_ref, came_ref, own_ref, up_ref, down_ref, far_up_ref, far_down_ref):
    far_up_ref[...] = kept_ref[2, 0:16, :] + came_ref[2, 0:16, :]
    far_down_ref[...] = kept_ref[2, 16:32, :] + came_ref[2, 16:32, :]
    own_ref[...] = kept_ref[0] + came_ref[0]
    up_ref[...] = kept_ref[1] + came_ref[1]
    down_ref[...] = kept_ref[3] + came_ref[3]


def pass_kernel(up_ref, down_ref, from_below_ref, from_above_ref, up_out_ref, down_out_ref):
    up_out_ref[0:16, :] = up_ref[0:16, :] + from_below_ref[...]
    up_out_ref[16:32, :] = up_ref[16:32, :]
    down_out_ref[0:16, :] = down_ref[0:16, :]
    down_out_ref[16:32, :] = down_ref[16:32, :] + from_above_ref[...]


def sum_kernel(own_ref, below_ref, above_ref, out_ref):
    out_ref[...] = own_ref[...] + below_ref[...] + above_ref[...]


def call(kernel, outs, scratch, homes):
    spaces = {"v": pltpu.VMEM, "h": pltpu.HBM}

    def shape(out):
        dims, dtype, kept = out
        return pltpu.VMEM(dims, dtype) if kept else jax.ShapeDtypeStruct(dims, dtype)

    def run(*operands):
        placed = [
            pltpu.with_memory_space_constraint(x, spaces[h]) if h in spaces else x for x, h in zip(operands, homes)
        ]
        return pl.pallas_call(
            kernel,
            out_shape=[shape(o) for o in outs],
            in_specs=[pl.BlockSpec(memory_space=pl.ANY if h == "h" else pltpu.VMEM) for h in homes],
            out_specs=[pl.BlockSpec(memory_space=pltpu.VMEM if o[2] is not None else pl.ANY) for o in outs],
            scratch_shapes=scratch,
            compiler_params=pltpu.CompilerParams(vmem_limit_bytes=12 * 2**20),
            cost_estimate=pl.CostEstimate(flops=0, bytes_accessed=0, transcendentals=0),
        )(*placed)

    return run


def share(value, axes, count):
    return lax.all_to_all(value, axes, 0, 0, tiled=True)


def shift(value, step, axis="y"):
    return lax.ppermute(value, axis, [(i, (i + step) % 4) for i in range(4)])


def scatter_sum(kept, sent):
    came = lax.ppermute(sent, "core", [(0, 1), (1, 0)])
    whole, half = ((32, COLS), f32, True), ((16, COLS), f32, True)
    own, up, down, far_up, far_down = call(pair_kernel, [whole, whole, whole, half, half], [], "vv")(kept, came)
    up, down = call(pass_kernel, [whole, whole], [], "vvvv")(up, down, shift(far_up, 1), shift(far_down, -1))
    (out,) = call(sum_kernel, [((32, COLS), f32, False)], [], "vvv")(own, shift(up, 1), shift(down, -1))
    return out


def on_device(student_codes, teacher_codes, prototypes):
    table, column = ((ROWS, COLS), f32, True), ((COL_TILES, LANES), f32, True)
    to_batch, to_proto = ((BATCHES, COL_TILES, LANES), f32, True), ((PROTOS, 1, FLAT), f32, True)
    crops, owned = ((ROW_TILES, LANES), f32, True), ((1, LANES), f32, True)
    lanes, row = pltpu.VMEM((ROWS, LANES), f32), pltpu.VMEM((ROW_TILES, LANES), f32)
    pay, protos = call(
        copy_kernel,
        [((ZS, 2 * OWN, WIDTH), bf16, True), ((WIDTH, COLS), f32, True)],
        [pltpu.VMEM((2, OWN, WIDTH), bf16), pltpu.SemaphoreType.DMA((3,))],
        "hhh",
    )(teacher_codes, student_codes, prototypes)
    block, inverse_row = ((BLOCK, WIDTH), bf16, True), ((1, COLS), f32, True)
    teacher, student = call(split_kernel, [block, block], [], "v")(share(pay, "z", ZS))
    low, inverse = call(norm_kernel, [((WIDTH, COLS), bf16, True), inverse_row], [], "vv")(protos, teacher)
    teachers = [teacher] + [shift(teacher, k, "x") for k in (1, 2, 3)]
    students = [student] + [shift(student, k, "x") for k in (1, 2, 3)]
    weights, mass = call(teacher_kernel, [table, inverse_row], [], "vvvvv")(*teachers, low)
    scores, grown, unit_t, extra, pay = call(
        student_kernel, [table, table, ((WIDTH, ROWS), bf16, True), crops, to_batch], [lanes], "vvvvvv"
    )(*students, low, mass)
    for iteration in range(ITERS - 1):
        first = iteration == 0
        (pay,) = call(functools.partial(row_kernel, first), [to_proto], [lanes, row], "vvv")(
            share(pay, BATCH, BATCHES), weights, extra
        )
        pay, extra = call(
            functools.partial(column_kernel, not first),
            [to_batch, owned if first else crops],
            [lanes, pltpu.VMEM((COL_TILES, LANES), f32)],
            "vv",
        )(share(pay, PROTO, PROTOS), weights)
    pay, column_scale = call(
        last_row_kernel,
        [to_proto, column],
        [lanes, lanes, pltpu.VMEM((2 * ROW_TILES, LANES), f32)],
        "vvv",
    )(share(pay, BATCH, BATCHES), weights, scores)
    kept, sent, own = call(
        grad_kernel,
        [((4, 32, COLS), f32, True), ((4, 32, COLS), f32, True), ((1, LANES), f32, False)],
        [lanes, lanes, row],
        "vvvvvvvv",
    )(share(pay, PROTO, PROTOS), weights, grown, column_scale, extra, unit_t, protos, inverse)
    return (scatter_sum(kept, sent), own[0, :OWN])


def solution(mesh):
    fine = Mesh(mesh.devices.reshape(4, 2, 8, 4), BATCH + PROTO)
    rows = P(BATCH + PROTO, None)
    return jax.shard_map(
        on_device,
        mesh=fine,
        in_specs=(rows, rows, P(None, PROTO)),
        out_specs=(P(BATCH, PROTO), P(BATCH + PROTO)),
        check_vma=False,
    )
```

```python
import functools

import jax
import jax.numpy as jnp
from jax import lax
from jax.experimental import pallas as pl
from jax.experimental.pallas import tpu as pltpu
from jax.sharding import Mesh, PartitionSpec as P

ITERS = 3

student_temp = 0.1
teacher_temp = 0.07
norm_eps = 1e-06
log2_e = 1.4426950408889634

BATCH = ("y", "core")
PROTO = ("z", "x")
BATCHES = 8
PROTOS = 32
ROWS = 1024
COLS = 2048
WIDTH = 256
LANES = 128
ROW_TILES = ROWS // LANES
COL_TILES = COLS // LANES
CHUNK = 256
WIDE = 512
FLAT = ROWS + LANES
OWN = ROWS // PROTOS
ZS = 8
XS = 4
BLOCK = ROWS // XS
f32 = jnp.float32
bf16 = jnp.bfloat16


def unit_rows(values):
    values = values.astype(f32)
    return values * lax.rsqrt(jnp.sum(values * values, axis=-1, keepdims=True) + norm_eps)


def row_of_lane_sums(parts_ref, out_row, pieces=ROW_TILES):
    for g in range(pieces):
        block = parts_ref[pl.ds(g * LANES, LANES), :]
        out_row(g, jnp.sum(block.T, axis=0, keepdims=True))


def column_of_row(row, out_ref):
    for g in range(ROW_TILES):
        out_ref[pl.ds(g * LANES, LANES), :] = jnp.broadcast_to(row[g : g + 1, :], (LANES, LANES)).T


def spread_columns(column_mass, pay_ref):
    row = jnp.concatenate([column_mass[:, t * LANES : (t + 1) * LANES] for t in range(COL_TILES)], axis=0)
    for k in range(BATCHES):
        pay_ref[k] = row


def block_place(q):
    step = lax.rem(q // 2 - lax.axis_index("y") + 4, 4)
    return jnp.where(lax.axis_index("core") == q % 2, 0, 4) + step


def block_rows(p):
    row = lax.rem(lax.axis_index("y") + p % 4, 4)
    core = lax.axis_index("core")
    return 2 * row + (core if p < 4 else 1 - core)


def owned_piece(row, k):
    z, x = k // XS, k % XS
    line = 2 * x + z // 4
    return pltpu.roll(row[line : line + 1, :], (LANES - (z % 4) * OWN) % LANES, 1)


def flat_row(row):
    return jnp.concatenate([row[g : g + 1, :] for g in range(ROW_TILES)], axis=1)


def flat_rows(flat):
    return jnp.concatenate([flat[:, g * LANES : (g + 1) * LANES] for g in range(ROW_TILES)], axis=0)


def copy_kernel(teacher_hbm, student_hbm, proto_hbm, pay_ref, proto_ref, codes_ref, sems):
    copies = [
        pltpu.make_async_copy(teacher_hbm, codes_ref.at[0], sems.at[0]),
        pltpu.make_async_copy(student_hbm, codes_ref.at[1], sems.at[1]),
        pltpu.make_async_copy(proto_hbm, proto_ref, sems.at[2]),
    ]
    for copy in copies:
        copy.start()
    copies[0].wait()
    copies[1].wait()
    for t in range(2):
        unit = unit_rows(codes_ref[t]).astype(bf16)
        for k in range(ZS):
            pay_ref[k, pl.ds(t * OWN, OWN), :] = unit
    copies[2].wait()


def split_kernel(came_ref, teacher_ref, student_ref):
    teacher_ref[...] = came_ref[:, 0:OWN, :].reshape(BLOCK, WIDTH)
    student_ref[...] = came_ref[:, OWN : 2 * OWN, :].reshape(BLOCK, WIDTH)


def norm_kernel(proto_ref, after_ref, low_ref, inverse_ref):
    for j in range(0, COLS, CHUNK):
        cols = pl.ds(j, CHUNK)
        piece = proto_ref[:, cols]
        inverse = lax.rsqrt(jnp.sum(piece * piece, axis=0, keepdims=True) + norm_eps)
        inverse_ref[:, cols] = inverse
        low_ref[:, cols] = (piece * inverse).astype(bf16)


def block_starts():
    x = lax.axis_index("x")
    return [pl.multiple_of(lax.rem(x + XS - k, XS) * BLOCK, BLOCK) for k in range(XS)]


def teacher_kernel(u0_ref, u1_ref, u2_ref, u3_ref, low_ref, weights_ref, mass_ref):
    starts = block_starts()

    for j in range(0, COLS, WIDE):
        cols = pl.ds(j, WIDE)
        low = low_ref[:, cols]
        mass = jnp.zeros((8, WIDE), f32)
        for unit_ref, start in zip((u0_ref, u1_ref, u2_ref, u3_ref), starts):
            scores = jnp.dot(unit_ref[...], low, preferred_element_type=f32)
            weights = jnp.exp2(scores * (log2_e / teacher_temp))
            weights_ref[pl.ds(start, BLOCK), cols] = weights
            mass = mass + jnp.sum(weights.reshape(BLOCK // 8, 8, WIDE), axis=0)
        mass_ref[:, cols] = jnp.sum(mass, axis=0, keepdims=True)


def student_kernel(
    u0_ref, u1_ref, u2_ref, u3_ref, low_ref, mass_ref, scores_ref, exp_ref, unit_t_ref, total_ref, pay_ref, parts_ref
):
    starts = block_starts()
    place = [pl.multiple_of(block_place(q) * 32, 32) for q in range(8)]
    units = (u0_ref, u1_ref, u2_ref, u3_ref)
    for unit_ref, start in zip(units, starts):
        turned = unit_ref[...].astype(f32).T.astype(bf16)
        for q in range(8):
            unit_t_ref[pl.ds(place[q], 32), pl.ds(start, BLOCK)] = turned[q * 32 : q * 32 + 32, :]
    parts_ref[...] = jnp.zeros_like(parts_ref)

    for j in range(0, COLS, WIDE):
        cols = pl.ds(j, WIDE)
        low = low_ref[:, cols]
        for unit_ref, start in zip(units, starts):
            rows = pl.ds(start, BLOCK)
            scores = jnp.dot(unit_ref[...], low, preferred_element_type=f32)
            scores_ref[rows, cols] = scores
            grown = jnp.exp2(scores * (log2_e / student_temp))
            exp_ref[rows, cols] = grown
            parts_ref[rows, :] += sum(grown[:, t : t + LANES] for t in range(LANES, WIDE, LANES)) + grown[:, :LANES]

    spread_columns(mass_ref[...], pay_ref)

    def put(g, row):
        total_ref[g : g + 1, :] = row

    row_of_lane_sums(parts_ref, put)


def scaled_rows(column, weights_ref, parts_ref, scores_ref=None, cross_ref=None):
    scale = [jnp.broadcast_to(column[t : t + 1, :], (8, LANES)) for t in range(COL_TILES)]

    for i in range(0, ROWS, 8):
        rows = pl.ds(i, 8)
        mass = cross = None
        for t in range(COL_TILES):
            cols = pl.ds(t * LANES, LANES)
            term = weights_ref[rows, cols] * scale[t]
            mass = term if mass is None else mass + term
            if scores_ref is not None:
                term = term * scores_ref[rows, cols]
                cross = term if cross is None else cross + term
        parts_ref[rows, :] = mass
        if scores_ref is not None:
            cross_ref[rows, :] = cross


def row_kernel(spread, mass_ref, weights_ref, extra_ref, pay_ref, parts_ref, row_ref):
    scaled_rows(1.0 / jnp.sum(mass_ref[...], axis=0), weights_ref, parts_ref)

    def put(g, row):
        row_ref[g : g + 1, :] = row

    row_of_lane_sums(parts_ref, put)
    flat, extra = flat_row(row_ref[...]), extra_ref[...]
    for k in range(PROTOS):
        pay_ref[k, :, 0:ROWS] = flat
        pay_ref[k, :, ROWS:FLAT] = owned_piece(extra, k) if spread else extra


def last_row_kernel(mass_ref, weights_ref, scores_ref, pay_ref, column_ref, parts_ref, cross_ref, row_ref):
    column = 1.0 / jnp.sum(mass_ref[...], axis=0)
    column_ref[...] = column
    scaled_rows(column, weights_ref, parts_ref, scores_ref, cross_ref)

    def put_mass(g, row):
        row_ref[g : g + 1, :] = row

    def put_cross(g, row):
        row_ref[ROW_TILES + g : ROW_TILES + g + 1, :] = row

    row_of_lane_sums(parts_ref, put_mass)
    row_of_lane_sums(cross_ref, put_cross)
    flat, cross = flat_row(row_ref[0:ROW_TILES, :]), row_ref[ROW_TILES : 2 * ROW_TILES, :]
    for k in range(PROTOS):
        pay_ref[k, :, 0:ROWS] = flat
        pay_ref[k, :, ROWS:FLAT] = owned_piece(cross, k)


def column_kernel(gather, mass_ref, weights_ref, pay_ref, extra_ref, scale_ref, sums_ref):
    sums = jnp.sum(mass_ref[...], axis=0)
    column_of_row(1.0 / flat_rows(sums), scale_ref)
    if gather:
        lane = lax.broadcasted_iota(jnp.int32, (1, LANES), 1)
        for g in range(ROW_TILES):
            row = jnp.zeros((1, LANES), f32)
            for t in range(4):
                piece = jnp.where(lane < OWN, mass_ref[(4 * (g % 2) + t) * XS + g // 2, :, ROWS:FLAT], 0.0)
                row = row + (pltpu.roll(piece, t * OWN, 1) if t else piece)
            extra_ref[g : g + 1, :] = row
    else:
        extra_ref[...] = sums[:, ROWS:FLAT]

    sums = [jnp.zeros((8, LANES), f32)] * COL_TILES
    for i in range(0, ROWS, 8):
        rows = pl.ds(i, 8)
        scale = scale_ref[rows, :]
        for t in range(COL_TILES):
            sums[t] = sums[t] + weights_ref[rows, pl.ds(t * LANES, LANES)] * scale
    for t in range(COL_TILES):
        sums_ref[t : t + 1, :] = jnp.sum(sums[t], axis=0, keepdims=True)
    row = sums_ref[...]
    for k in range(BATCHES):
        pay_ref[k] = row


def grad_kernel(
    mass_ref,
    weights_ref,
    exp_ref,
    column_ref,
    total_ref,
    unit_t_ref,
    proto_ref,
    inverse_ref,
    kept_ref,
    sent_ref,
    own_ref,
    prob_ref,
    target_ref,
    row_ref,
):
    sums = jnp.sum(mass_ref[...], axis=0)
    row_ref[...] = 1.0 / flat_rows(sums)
    factor = 1.0 / (student_temp * ROWS * BATCHES)
    column_of_row(factor / total_ref[...], prob_ref)
    column_of_row(factor * row_ref[...], target_ref)
    z = lax.axis_index("z")
    line, turn = pl.ds(2 * lax.axis_index("x") + z // 4, 1), LANES - lax.rem(z, 4) * OWN
    row_scale = pltpu.roll(row_ref[line, :], turn, 1)
    total = pltpu.roll(total_ref[line, :], turn, 1)
    own_ref[...] = jnp.log(total) - sums[:, ROWS:FLAT] * row_scale * (1.0 / student_temp)
    blocks = [pl.multiple_of(block_rows(p) * 32, 32) for p in range(8)]
    for j in range(COLS // CHUNK):
        cols = pl.ds(j * CHUNK, CHUNK)
        pieces = []
        for t in range(2):
            part = pl.ds(j * CHUNK + t * LANES, LANES)
            scale = column_ref[2 * j + t : 2 * j + t + 1, :]
            pieces.append(
                (exp_ref[:, part] * prob_ref[...] - weights_ref[:, part] * scale * target_ref[...]).astype(bf16)
            )
        score_grad = jnp.concatenate(pieces, axis=1)
        grad = jnp.dot(unit_t_ref[...], score_grad, preferred_element_type=f32)
        inverse = inverse_ref[:, cols]
        directions = jnp.concatenate([proto_ref[pl.ds(b, 32), cols] for b in blocks], axis=0) * inverse
        radial = jnp.sum(directions * grad, axis=0, keepdims=True)
        full = (grad - directions * radial) * inverse
        for s in range(4):
            kept_ref[s, :, cols] = full[s * 32 : s * 32 + 32, :]
            sent_ref[s, :, cols] = full[128 + s * 32 : 160 + s * 32, :]


def pair_kernel(kept_ref, came_ref, own_ref, up_ref, down_ref, far_up_ref, far_down_ref):
    far_up_ref[...] = kept_ref[2, 0:16, :] + came_ref[2, 0:16, :]
    far_down_ref[...] = kept_ref[2, 16:32, :] + came_ref[2, 16:32, :]
    own_ref[...] = kept_ref[0] + came_ref[0]
    up_ref[...] = kept_ref[1] + came_ref[1]
    down_ref[...] = kept_ref[3] + came_ref[3]


def pass_kernel(up_ref, down_ref, from_below_ref, from_above_ref, up_out_ref, down_out_ref):
    up_out_ref[0:16, :] = up_ref[0:16, :] + from_below_ref[...]
    up_out_ref[16:32, :] = up_ref[16:32, :]
    down_out_ref[0:16, :] = down_ref[0:16, :]
    down_out_ref[16:32, :] = down_ref[16:32, :] + from_above_ref[...]


def sum_kernel(own_ref, below_ref, above_ref, out_ref):
    out_ref[...] = own_ref[...] + below_ref[...] + above_ref[...]


def call(kernel, outs, scratch, homes):
    spaces = {"v": pltpu.VMEM, "h": pltpu.HBM}

    def shape(out):
        dims, dtype, kept = out
        return pltpu.VMEM(dims, dtype) if kept else jax.ShapeDtypeStruct(dims, dtype)

    def run(*operands):
        placed = [
            pltpu.with_memory_space_constraint(x, spaces[h]) if h in spaces else x for x, h in zip(operands, homes)
        ]
        return pl.pallas_call(
            kernel,
            out_shape=[shape(o) for o in outs],
            in_specs=[pl.BlockSpec(memory_space=pl.ANY if h == "h" else pltpu.VMEM) for h in homes],
            out_specs=[pl.BlockSpec(memory_space=pltpu.VMEM if o[2] is not None else pl.ANY) for o in outs],
            scratch_shapes=scratch,
            compiler_params=pltpu.CompilerParams(vmem_limit_bytes=12 * 2**20),
            cost_estimate=pl.CostEstimate(flops=0, bytes_accessed=0, transcendentals=0),
        )(*placed)

    return run


def share(value, axes, count):
    return lax.all_to_all(value, axes, 0, 0, tiled=True)


def shift(value, step, axis="y"):
    return lax.ppermute(value, axis, [(i, (i + step) % 4) for i in range(4)])


def scatter_sum(kept, sent):
    came = lax.ppermute(sent, "core", [(0, 1), (1, 0)])
    whole, half = ((32, COLS), f32, True), ((16, COLS), f32, True)
    own, up, down, far_up, far_down = call(pair_kernel, [whole, whole, whole, half, half], [], "vv")(kept, came)
    up, down = call(pass_kernel, [whole, whole], [], "vvvv")(up, down, shift(far_up, 1), shift(far_down, -1))
    (out,) = call(sum_kernel, [((32, COLS), f32, False)], [], "vvv")(own, shift(up, 1), shift(down, -1))
    return out


def on_device(student_codes, teacher_codes, prototypes):
    table, column = ((ROWS, COLS), f32, True), ((COL_TILES, LANES), f32, True)
    to_batch, to_proto = ((BATCHES, COL_TILES, LANES), f32, True), ((PROTOS, 1, FLAT), f32, True)
    crops, owned = ((ROW_TILES, LANES), f32, True), ((1, LANES), f32, True)
    lanes, row = pltpu.VMEM((ROWS, LANES), f32), pltpu.VMEM((ROW_TILES, LANES), f32)
    pay, protos = call(
        copy_kernel,
        [((ZS, 2 * OWN, WIDTH), bf16, True), ((WIDTH, COLS), f32, True)],
        [pltpu.VMEM((2, OWN, WIDTH), bf16), pltpu.SemaphoreType.DMA((3,))],
        "hhh",
    )(teacher_codes, student_codes, prototypes)
    block, inverse_row = ((BLOCK, WIDTH), bf16, True), ((1, COLS), f32, True)
    teacher, student = call(split_kernel, [block, block], [], "v")(share(pay, "z", ZS))
    low, inverse = call(norm_kernel, [((WIDTH, COLS), bf16, True), inverse_row], [], "vv")(protos, teacher)
    teachers = [teacher] + [shift(teacher, k, "x") for k in (1, 2, 3)]
    students = [student] + [shift(student, k, "x") for k in (1, 2, 3)]
    weights, mass = call(teacher_kernel, [table, inverse_row], [], "vvvvv")(*teachers, low)
    scores, grown, unit_t, extra, pay = call(
        student_kernel, [table, table, ((WIDTH, ROWS), bf16, True), crops, to_batch], [lanes], "vvvvvv"
    )(*students, low, mass)
    for iteration in range(ITERS - 1):
        first = iteration == 0
        (pay,) = call(functools.partial(row_kernel, first), [to_proto], [lanes, row], "vvv")(
            share(pay, BATCH, BATCHES), weights, extra
        )
        pay, extra = call(
            functools.partial(column_kernel, not first),
            [to_batch, owned if first else crops],
            [lanes, pltpu.VMEM((COL_TILES, LANES), f32)],
            "vv",
        )(share(pay, PROTO, PROTOS), weights)
    pay, column_scale = call(
        last_row_kernel,
        [to_proto, column],
        [lanes, lanes, pltpu.VMEM((2 * ROW_TILES, LANES), f32)],
        "vvv",
    )(share(pay, BATCH, BATCHES), weights, scores)
    kept, sent, own = call(
        grad_kernel,
        [((4, 32, COLS), f32, True), ((4, 32, COLS), f32, True), ((1, LANES), f32, False)],
        [lanes, lanes, row],
        "vvvvvvvv",
    )(share(pay, PROTO, PROTOS), weights, grown, column_scale, extra, unit_t, protos, inverse)
    return (scatter_sum(kept, sent), own[0, :OWN])


def solution(mesh):
    fine = Mesh(mesh.devices.reshape(4, 2, 8, 4), BATCH + PROTO)
    rows = P(BATCH + PROTO, None)
    return jax.shard_map(
        on_device,
        mesh=fine,
        in_specs=(rows, rows, P(None, PROTO)),
        out_specs=(P(BATCH, PROTO), P(BATCH + PROTO)),
        check_vma=False,
    )
```

```python
import functools

import jax
import jax.numpy as jnp
from jax import lax
from jax.experimental import pallas as pl
from jax.experimental.pallas import tpu as pltpu
from jax.sharding import Mesh, PartitionSpec as P

ITERS = 3

student_temp = 0.1
teacher_temp = 0.07
norm_eps = 1e-06
log2_e = 1.4426950408889634

BATCH = ("y", "core")
PROTO = ("z", "x")
BATCHES = 8
PROTOS = 32
ROWS = 1024
COLS = 2048
WIDTH = 256
LANES = 128
ROW_TILES = ROWS // LANES
COL_TILES = COLS // LANES
CHUNK = 256
WIDE = 512
HEAD = 14.0
FLAT = ROWS + LANES
OWN = ROWS // PROTOS
ZS = 8
XS = 4
BLOCK = ROWS // XS
f32 = jnp.float32
bf16 = jnp.bfloat16


def unit_rows(values):
    values = values.astype(f32)
    return values * lax.rsqrt(jnp.sum(values * values, axis=-1, keepdims=True) + norm_eps)


def row_of_lane_sums(parts_ref, out_row, pieces=ROW_TILES):
    for g in range(pieces):
        block = parts_ref[pl.ds(g * LANES, LANES), :]
        out_row(g, jnp.sum(block.T, axis=0, keepdims=True))


def column_of_row(row, out_ref):
    for g in range(ROW_TILES):
        out_ref[pl.ds(g * LANES, LANES), :] = jnp.broadcast_to(row[g : g + 1, :], (LANES, LANES)).T


def spread_columns(column_mass, pay_ref):
    row = jnp.concatenate([column_mass[:, t * LANES : (t + 1) * LANES] for t in range(COL_TILES)], axis=0)
    for k in range(BATCHES):
        pay_ref[k] = row


def block_place(q):
    step = lax.rem(q // 2 - lax.axis_index("y") + 4, 4)
    return jnp.where(lax.axis_index("core") == q % 2, 0, 4) + step


def block_rows(p):
    row = lax.rem(lax.axis_index("y") + p % 4, 4)
    core = lax.axis_index("core")
    return 2 * row + (core if p < 4 else 1 - core)


def owned_piece(row, k):
    z, x = k // XS, k % XS
    line = 2 * x + z // 4
    return pltpu.roll(row[line : line + 1, :], (LANES - (z % 4) * OWN) % LANES, 1)


def flat_row(row):
    return jnp.concatenate([row[g : g + 1, :] for g in range(ROW_TILES)], axis=1)


def flat_rows(flat):
    return jnp.concatenate([flat[:, g * LANES : (g + 1) * LANES] for g in range(ROW_TILES)], axis=0)


def copy_kernel(teacher_hbm, student_hbm, pay_ref, codes_ref, sems):
    copies = [
        pltpu.make_async_copy(teacher_hbm, codes_ref.at[0], sems.at[0]),
        pltpu.make_async_copy(student_hbm, codes_ref.at[1], sems.at[1]),
    ]
    for copy in copies:
        copy.start()
    for copy in copies:
        copy.wait()
    for t in range(2):
        unit = unit_rows(codes_ref[t]).astype(bf16)
        for k in range(ZS):
            pay_ref[k, pl.ds(t * OWN, OWN), :] = unit


def split_kernel(came_ref, teacher_ref, student_ref):
    teacher_ref[...] = came_ref[:, 0:OWN, :].reshape(BLOCK, WIDTH)
    student_ref[...] = came_ref[:, OWN : 2 * OWN, :].reshape(BLOCK, WIDTH)


def norm_kernel(proto_hbm, after_ref, low_ref, inverse_ref, proto_ref, sems):
    copies = [
        pltpu.make_async_copy(proto_hbm.at[:, pl.ds(j, WIDE)], proto_ref.at[:, pl.ds(j, WIDE)], sems.at[j // WIDE])
        for j in range(0, COLS, WIDE)
    ]
    for copy in copies:
        copy.start()
    for j in range(0, COLS, WIDE):
        copies[j // WIDE].wait()
        cols = pl.ds(j, WIDE)
        piece = proto_ref[:, cols]
        inverse = lax.rsqrt(jnp.sum(piece * piece, axis=0, keepdims=True) + norm_eps)
        inverse_ref[:, cols] = inverse
        low_ref[:, cols] = (piece * inverse).astype(bf16)


def block_starts():
    x = lax.axis_index("x")
    return [pl.multiple_of(lax.rem(x + XS - k, XS) * BLOCK, BLOCK) for k in range(XS)]


def teacher_kernel(u0_ref, u1_ref, u2_ref, u3_ref, low_ref, weights_ref, mass_ref):
    units, starts = (u0_ref, u1_ref, u2_ref, u3_ref), block_starts()

    for j in range(0, COLS, WIDE):
        cols = pl.ds(j, WIDE)
        low = low_ref[:, cols]
        mass = jnp.zeros((8, WIDE), f32)
        for unit_ref, start in zip(units, starts):
            scores = jnp.dot(unit_ref[...], low, preferred_element_type=f32)
            weights = jnp.exp2(scores * (log2_e / teacher_temp))
            weights_ref[pl.ds(start, BLOCK), cols] = weights
            mass = mass + jnp.sum(weights.reshape(BLOCK // 8, 8, WIDE), axis=0)
        mass_ref[:, cols] = jnp.sum(mass, axis=0, keepdims=True)


def student_kernel(
    u0_ref,
    u1_ref,
    u2_ref,
    u3_ref,
    low_ref,
    mass_ref,
    scores_ref,
    exp_ref,
    unit_t_ref,
    total_ref,
    pay_ref,
    parts_ref,
):
    units, starts = (u0_ref, u1_ref, u2_ref, u3_ref), block_starts()
    place = [pl.multiple_of(block_place(q) * 32, 32) for q in range(8)]
    for unit_ref, start in zip(units, starts):
        turned = unit_ref[...].astype(f32).T.astype(bf16)
        for q in range(8):
            unit_t_ref[pl.ds(place[q], 32), pl.ds(start, BLOCK)] = turned[q * 32 : q * 32 + 32, :]
    parts_ref[...] = jnp.zeros_like(parts_ref)

    for j in range(0, COLS, WIDE):
        cols = pl.ds(j, WIDE)
        low = low_ref[:, cols]
        for unit_ref, start in zip(units, starts):
            rows = pl.ds(start, BLOCK)
            scores = jnp.dot(unit_ref[...], low, preferred_element_type=f32)
            scores_ref[rows, cols] = scores
            grown = jnp.exp2(scores * (log2_e / student_temp))
            exp_ref[rows, cols] = grown
            parts_ref[rows, :] += sum(grown[:, t : t + LANES] for t in range(LANES, WIDE, LANES)) + grown[:, :LANES]

    spread_columns(mass_ref[...], pay_ref)

    def put(g, row):
        total_ref[g : g + 1, :] = row

    row_of_lane_sums(parts_ref, put)


def scaled_rows(column, weights_ref, parts_ref, scores_ref=None, cross_ref=None):
    scale = [jnp.broadcast_to(column[t : t + 1, :], (8, LANES)) for t in range(COL_TILES)]

    for i in range(0, ROWS, 8):
        rows = pl.ds(i, 8)
        mass = cross = None
        for t in range(COL_TILES):
            cols = pl.ds(t * LANES, LANES)
            term = weights_ref[rows, cols] * scale[t]
            mass = term if mass is None else mass + term
            if scores_ref is not None:
                term = term * scores_ref[rows, cols]
                cross = term if cross is None else cross + term
        parts_ref[rows, :] = mass
        if scores_ref is not None:
            cross_ref[rows, :] = cross


def row_kernel(spread, mass_ref, weights_ref, extra_ref, pay_ref, parts_ref, row_ref):
    scaled_rows(1.0 / jnp.sum(mass_ref[...], axis=0), weights_ref, parts_ref)

    def put(g, row):
        row_ref[g : g + 1, :] = row

    row_of_lane_sums(parts_ref, put)
    flat, extra = flat_row(row_ref[...]), extra_ref[...]
    for k in range(PROTOS):
        pay_ref[k, :, 0:ROWS] = flat
        pay_ref[k, :, ROWS:FLAT] = owned_piece(extra, k) if spread else extra


def last_row_kernel(mass_ref, weights_ref, scores_ref, pay_ref, column_ref, parts_ref, cross_ref, row_ref):
    column = 1.0 / jnp.sum(mass_ref[...], axis=0)
    column_ref[...] = column
    scaled_rows(column, weights_ref, parts_ref, scores_ref, cross_ref)

    def put_mass(g, row):
        row_ref[g : g + 1, :] = row

    def put_cross(g, row):
        row_ref[ROW_TILES + g : ROW_TILES + g + 1, :] = row

    row_of_lane_sums(parts_ref, put_mass)
    row_of_lane_sums(cross_ref, put_cross)
    flat, cross = flat_row(row_ref[0:ROW_TILES, :]), row_ref[ROW_TILES : 2 * ROW_TILES, :]
    for k in range(PROTOS):
        pay_ref[k, :, 0:ROWS] = flat
        pay_ref[k, :, ROWS:FLAT] = owned_piece(cross, k)


def column_kernel(gather, mass_ref, weights_ref, pay_ref, extra_ref, scale_ref, sums_ref):
    sums = jnp.sum(mass_ref[...], axis=0)
    column_of_row(1.0 / flat_rows(sums), scale_ref)
    if gather:
        lane = lax.broadcasted_iota(jnp.int32, (1, LANES), 1)
        for g in range(ROW_TILES):
            row = jnp.zeros((1, LANES), f32)
            for t in range(4):
                piece = jnp.where(lane < OWN, mass_ref[(4 * (g % 2) + t) * XS + g // 2, :, ROWS:FLAT], 0.0)
                row = row + (pltpu.roll(piece, t * OWN, 1) if t else piece)
            extra_ref[g : g + 1, :] = row
    else:
        extra_ref[...] = sums[:, ROWS:FLAT]

    sums = [jnp.zeros((8, LANES), f32)] * COL_TILES
    for i in range(0, ROWS, 8):
        rows = pl.ds(i, 8)
        scale = scale_ref[rows, :]
        for t in range(COL_TILES):
            sums[t] = sums[t] + weights_ref[rows, pl.ds(t * LANES, LANES)] * scale
    for t in range(COL_TILES):
        sums_ref[t : t + 1, :] = jnp.sum(sums[t], axis=0, keepdims=True)
    row = sums_ref[...]
    for k in range(BATCHES):
        pay_ref[k] = row


def grad_kernel(
    mass_ref,
    weights_ref,
    exp_ref,
    column_ref,
    total_ref,
    unit_t_ref,
    proto_ref,
    inverse_ref,
    kept_ref,
    sent_ref,
    own_ref,
    prob_ref,
    target_ref,
    row_ref,
):
    sums = jnp.sum(mass_ref[...], axis=0)
    row_ref[...] = 1.0 / flat_rows(sums)
    factor = 1.0 / (student_temp * ROWS * BATCHES)
    column_of_row(factor / total_ref[...], prob_ref)
    column_of_row(factor * row_ref[...], target_ref)
    z = lax.axis_index("z")
    line, turn = pl.ds(2 * lax.axis_index("x") + z // 4, 1), LANES - lax.rem(z, 4) * OWN
    row_scale = pltpu.roll(row_ref[line, :], turn, 1)
    total = pltpu.roll(total_ref[line, :], turn, 1)
    own_ref[...] = jnp.log(total) - sums[:, ROWS:FLAT] * row_scale * (1.0 / student_temp)
    blocks = [pl.multiple_of(block_rows(p) * 32, 32) for p in range(8)]
    for j in range(COLS // CHUNK):
        cols = pl.ds(j * CHUNK, CHUNK)
        pieces = []
        for t in range(2):
            part = pl.ds(j * CHUNK + t * LANES, LANES)
            scale = column_ref[2 * j + t : 2 * j + t + 1, :]
            pieces.append(
                (exp_ref[:, part] * prob_ref[...] - weights_ref[:, part] * scale * target_ref[...]).astype(bf16)
            )
        score_grad = jnp.concatenate(pieces, axis=1)
        grad = jnp.dot(unit_t_ref[...], score_grad, preferred_element_type=f32)
        inverse = inverse_ref[:, cols]
        directions = jnp.concatenate([proto_ref[pl.ds(b, 32), cols] for b in blocks], axis=0) * inverse
        radial = jnp.sum(directions * grad, axis=0, keepdims=True)
        full = (grad - directions * radial) * inverse
        for s in range(4):
            kept_ref[s, :, cols] = full[s * 32 : s * 32 + 32, :]
            sent_ref[s, :, cols] = full[128 + s * 32 : 160 + s * 32, :]


def pair_kernel(kept_ref, came_ref, own_ref, *out_refs):
    for s, out_ref in zip((2, 1, 3), out_refs):
        exponents = []
        for t in range(COL_TILES):
            cols = pl.ds(t * LANES, LANES)
            value = kept_ref[s, :, cols] + came_ref[s, :, cols]
            top = jnp.max(jnp.abs(value), axis=0, keepdims=True)
            exponent = jnp.clip(jnp.ceil(jnp.log2(top)), -100.0, 120.0)
            out_ref[:, cols] = value * jnp.exp2(HEAD - exponent)
            exponents.append(exponent)
        out_ref[0:16, COLS:] = jnp.concatenate(exponents, axis=0)
        out_ref[16:32, COLS:] = jnp.zeros((16, LANES), f32)
    own_ref[...] = kept_ref[0] + came_ref[0]


def sum_kernel(own_ref, first_ref, second_ref, third_ref, out_ref):
    scales = [jnp.exp2(ref[0:16, COLS:] - HEAD) for ref in (first_ref, second_ref, third_ref)]
    for t in range(COL_TILES):
        cols = pl.ds(t * LANES, LANES)
        value = own_ref[:, cols]
        for ref, scale in zip((first_ref, second_ref, third_ref), scales):
            value = value + ref[:, cols] * scale[t : t + 1, :]
        out_ref[:, cols] = value


def call(kernel, outs, scratch, homes):
    spaces = {"v": pltpu.VMEM, "h": pltpu.HBM}

    def shape(out):
        dims, dtype, kept = out
        return pltpu.VMEM(dims, dtype) if kept else jax.ShapeDtypeStruct(dims, dtype)

    def run(*operands):
        placed = [
            pltpu.with_memory_space_constraint(x, spaces[h]) if h in spaces else x for x, h in zip(operands, homes)
        ]
        return pl.pallas_call(
            kernel,
            out_shape=[shape(o) for o in outs],
            in_specs=[pl.BlockSpec(memory_space=pl.ANY if h == "h" else pltpu.VMEM) for h in homes],
            out_specs=[pl.BlockSpec(memory_space=pltpu.VMEM if o[2] is not None else pl.ANY) for o in outs],
            scratch_shapes=scratch,
            compiler_params=pltpu.CompilerParams(vmem_limit_bytes=12 * 2**20),
            cost_estimate=pl.CostEstimate(flops=0, bytes_accessed=0, transcendentals=0),
        )(*placed)

    return run


def share(value, axes, count):
    return lax.all_to_all(value, axes, 0, 0, tiled=True)


def shift(value, step, axis="y"):
    return lax.ppermute(value, axis, [(i, (i + step) % 4) for i in range(4)])


def scatter_sum(kept, sent):
    came = lax.ppermute(sent, "core", [(0, 1), (1, 0)])
    out = ((32, COLS + LANES), f32, True)
    own, *blocks = call(pair_kernel, [((32, COLS), f32, True), out, out, out], [], "vv")(kept, came)
    came = [shift(block.astype(jnp.float16), k).astype(f32) for block, k in zip(blocks, (2, 1, 3))]
    (total,) = call(sum_kernel, [((32, COLS), f32, False)], [], "vvvv")(own, *came)
    return total


def on_device(student_codes, teacher_codes, prototypes):
    table, column = ((ROWS, COLS), f32, True), ((COL_TILES, LANES), f32, True)
    to_batch, to_proto = ((BATCHES, COL_TILES, LANES), f32, True), ((PROTOS, 1, FLAT), f32, True)
    crops, owned = ((ROW_TILES, LANES), f32, True), ((1, LANES), f32, True)
    lanes, row = pltpu.VMEM((ROWS, LANES), f32), pltpu.VMEM((ROW_TILES, LANES), f32)
    (pay,) = call(
        copy_kernel,
        [((ZS, 2 * OWN, WIDTH), bf16, True)],
        [pltpu.VMEM((2, OWN, WIDTH), bf16), pltpu.SemaphoreType.DMA((2,))],
        "hh",
    )(teacher_codes, student_codes)
    block, inverse_row = ((BLOCK, WIDTH), bf16, True), ((1, COLS), f32, True)
    teacher, student = call(split_kernel, [block, block], [], "v")(share(pay, "z", ZS))
    low, inverse, protos = call(
        norm_kernel,
        [((WIDTH, COLS), bf16, True), inverse_row, ((WIDTH, COLS), f32, True)],
        [pltpu.SemaphoreType.DMA((COLS // WIDE,))],
        "hv",
    )(prototypes, teacher)
    teachers = [teacher] + [shift(teacher, k, "x") for k in (1, 2, 3)]
    above = shift(student, 3, "x")
    students = [student, shift(student, 1, "x"), shift(above, 3, "x"), above]
    weights, mass = call(teacher_kernel, [table, inverse_row], [], "vvvvv")(*teachers, low)
    scores, grown, unit_t, extra, pay = call(
        student_kernel, [table, table, ((WIDTH, ROWS), bf16, True), crops, to_batch], [lanes], "vvvvvv"
    )(*students, low, mass)
    for iteration in range(ITERS - 1):
        first = iteration == 0
        (pay,) = call(functools.partial(row_kernel, first), [to_proto], [lanes, row], "vvv")(
            share(pay, BATCH, BATCHES), weights, extra
        )
        pay, extra = call(
            functools.partial(column_kernel, not first),
            [to_batch, owned if first else crops],
            [lanes, pltpu.VMEM((COL_TILES, LANES), f32)],
            "vv",
        )(share(pay, PROTO, PROTOS), weights)
    pay, column_scale = call(
        last_row_kernel,
        [to_proto, column],
        [lanes, lanes, pltpu.VMEM((2 * ROW_TILES, LANES), f32)],
        "vvv",
    )(share(pay, BATCH, BATCHES), weights, scores)
    kept, sent, own = call(
        grad_kernel,
        [((4, 32, COLS), f32, True), ((4, 32, COLS), f32, True), ((1, LANES), f32, False)],
        [lanes, lanes, row],
        "vvvvvvvv",
    )(share(pay, PROTO, PROTOS), weights, grown, column_scale, extra, unit_t, protos, inverse)
    return (scatter_sum(kept, sent), own[0, :OWN])


def solution(mesh):
    fine = Mesh(mesh.devices.reshape(4, 2, 8, 4), BATCH + PROTO)
    rows = P(BATCH + PROTO, None)
    return jax.shard_map(
        on_device,
        mesh=fine,
        in_specs=(rows, rows, P(None, PROTO)),
        out_specs=(P(BATCH, PROTO), P(BATCH + PROTO)),
        check_vma=False,
    )
```

```python
import functools

import jax
import jax.numpy as jnp
from jax import lax
from jax.experimental import pallas as pl
from jax.experimental.pallas import tpu as pltpu
from jax.sharding import Mesh, PartitionSpec as P

ITERS = 3

student_temp = 0.1
teacher_temp = 0.07
norm_eps = 1e-06
log2_e = 1.4426950408889634

BATCH = ("y", "core")
PROTO = ("z", "x")
BATCHES = 8
PROTOS = 32
ROWS = 1024
COLS = 2048
WIDTH = 256
LANES = 128
ROW_TILES = ROWS // LANES
COL_TILES = COLS // LANES
CHUNK = 256
WIDE = 512
HALF = COLS // 2
HEAD = 14.0
FLAT = ROWS + LANES
OWN = ROWS // PROTOS
ZS = 8
XS = 4
BLOCK = ROWS // XS
f32 = jnp.float32
bf16 = jnp.bfloat16


def unit_rows(values):
    values = values.astype(f32)
    return values * lax.rsqrt(jnp.sum(values * values, axis=-1, keepdims=True) + norm_eps)


def row_of_lane_sums(parts_ref, out_row, pieces=ROW_TILES):
    for g in range(pieces):
        block = parts_ref[pl.ds(g * LANES, LANES), :]
        out_row(g, jnp.sum(block.T, axis=0, keepdims=True))


def column_of_row(row, out_ref):
    for g in range(ROW_TILES):
        out_ref[pl.ds(g * LANES, LANES), :] = jnp.broadcast_to(row[g : g + 1, :], (LANES, LANES)).T


def spread_columns(column_mass, pay_ref):
    row = jnp.concatenate([column_mass[:, t * LANES : (t + 1) * LANES] for t in range(COL_TILES)], axis=0)
    for k in range(BATCHES):
        pay_ref[k] = row


def block_place(q):
    step = lax.rem(q // 2 - lax.axis_index("y") + 4, 4)
    return jnp.where(lax.axis_index("core") == q % 2, 0, 4) + step


def block_rows(p):
    row = lax.rem(lax.axis_index("y") + p % 4, 4)
    core = lax.axis_index("core")
    return 2 * row + (core if p < 4 else 1 - core)


def owned_piece(row, k):
    z, x = k // XS, k % XS
    line = 2 * x + z // 4
    return pltpu.roll(row[line : line + 1, :], (LANES - (z % 4) * OWN) % LANES, 1)


def flat_row(row):
    return jnp.concatenate([row[g : g + 1, :] for g in range(ROW_TILES)], axis=1)


def flat_rows(flat):
    return jnp.concatenate([flat[:, g * LANES : (g + 1) * LANES] for g in range(ROW_TILES)], axis=0)


def copy_kernel(teacher_hbm, student_hbm, pay_ref, codes_ref, sems):
    copies = [
        pltpu.make_async_copy(teacher_hbm, codes_ref.at[0], sems.at[0]),
        pltpu.make_async_copy(student_hbm, codes_ref.at[1], sems.at[1]),
    ]
    for copy in copies:
        copy.start()
    for copy in copies:
        copy.wait()
    for t in range(2):
        unit = unit_rows(codes_ref[t]).astype(bf16)
        for k in range(ZS):
            pay_ref[k, pl.ds(t * OWN, OWN), :] = unit


def split_kernel(came_ref, teacher_ref, student_ref):
    teacher_ref[...] = came_ref[:, 0:OWN, :].reshape(BLOCK, WIDTH)
    student_ref[...] = came_ref[:, OWN : 2 * OWN, :].reshape(BLOCK, WIDTH)


def norm_kernel(proto_hbm, after_ref, low_ref, inverse_ref, proto_ref, sems):
    copies = [
        pltpu.make_async_copy(proto_hbm.at[:, pl.ds(j, WIDE)], proto_ref.at[:, pl.ds(j, WIDE)], sems.at[j // WIDE])
        for j in range(0, COLS, WIDE)
    ]
    for copy in copies:
        copy.start()
    for j in range(0, COLS, WIDE):
        copies[j // WIDE].wait()
        cols = pl.ds(j, WIDE)
        piece = proto_ref[:, cols]
        inverse = lax.rsqrt(jnp.sum(piece * piece, axis=0, keepdims=True) + norm_eps)
        inverse_ref[:, cols] = inverse
        low_ref[:, cols] = (piece * inverse).astype(bf16)


def block_starts():
    x = lax.axis_index("x")
    return [pl.multiple_of(lax.rem(x + XS - k, XS) * BLOCK, BLOCK) for k in range(XS)]


def teacher_kernel(u0_ref, u1_ref, u2_ref, u3_ref, low_ref, weights_ref, mass_ref):
    units, starts = (u0_ref, u1_ref, u2_ref, u3_ref), block_starts()

    for j in range(0, COLS, WIDE):
        cols = pl.ds(j, WIDE)
        low = low_ref[:, cols]
        mass = jnp.zeros((8, WIDE), f32)
        for unit_ref, start in zip(units, starts):
            scores = jnp.dot(unit_ref[...], low, preferred_element_type=f32)
            weights = jnp.exp2(scores * (log2_e / teacher_temp))
            weights_ref[pl.ds(start, BLOCK), cols] = weights
            mass = mass + jnp.sum(weights.reshape(BLOCK // 8, 8, WIDE), axis=0)
        mass_ref[:, cols] = jnp.sum(mass, axis=0, keepdims=True)


def student_kernel(
    u0_ref,
    u1_ref,
    u2_ref,
    u3_ref,
    low_ref,
    mass_ref,
    scores_ref,
    exp_ref,
    unit_t_ref,
    total_ref,
    pay_ref,
    parts_ref,
):
    units, starts = (u0_ref, u1_ref, u2_ref, u3_ref), block_starts()
    place = [pl.multiple_of(block_place(q) * 32, 32) for q in range(8)]
    for unit_ref, start in zip(units, starts):
        turned = unit_ref[...].astype(f32).T.astype(bf16)
        for q in range(8):
            unit_t_ref[pl.ds(place[q], 32), pl.ds(start, BLOCK)] = turned[q * 32 : q * 32 + 32, :]
    parts_ref[...] = jnp.zeros_like(parts_ref)

    for j in range(0, COLS, WIDE):
        cols = pl.ds(j, WIDE)
        low = low_ref[:, cols]
        for unit_ref, start in zip(units, starts):
            rows = pl.ds(start, BLOCK)
            scores = jnp.dot(unit_ref[...], low, preferred_element_type=f32)
            scores_ref[rows, cols] = scores
            grown = jnp.exp2(scores * (log2_e / student_temp))
            exp_ref[rows, cols] = grown
            parts_ref[rows, :] += sum(grown[:, t : t + LANES] for t in range(LANES, WIDE, LANES)) + grown[:, :LANES]

    spread_columns(mass_ref[...], pay_ref)

    def put(g, row):
        total_ref[g : g + 1, :] = row

    row_of_lane_sums(parts_ref, put)


def scaled_rows(column, weights_ref, parts_ref, scores_ref=None, cross_ref=None):
    scale = [jnp.broadcast_to(column[t : t + 1, :], (8, LANES)) for t in range(COL_TILES)]

    for i in range(0, ROWS, 8):
        rows = pl.ds(i, 8)
        mass = cross = None
        for t in range(COL_TILES):
            cols = pl.ds(t * LANES, LANES)
            term = weights_ref[rows, cols] * scale[t]
            mass = term if mass is None else mass + term
            if scores_ref is not None:
                term = term * scores_ref[rows, cols]
                cross = term if cross is None else cross + term
        parts_ref[rows, :] = mass
        if scores_ref is not None:
            cross_ref[rows, :] = cross


def row_kernel(spread, mass_ref, weights_ref, extra_ref, pay_ref, parts_ref, row_ref):
    scaled_rows(1.0 / jnp.sum(mass_ref[...], axis=0), weights_ref, parts_ref)

    def put(g, row):
        row_ref[g : g + 1, :] = row

    row_of_lane_sums(parts_ref, put)
    flat, extra = flat_row(row_ref[...]), extra_ref[...]
    for k in range(PROTOS):
        pay_ref[k, :, 0:ROWS] = flat
        pay_ref[k, :, ROWS:FLAT] = owned_piece(extra, k) if spread else extra


def last_row_kernel(mass_ref, weights_ref, scores_ref, pay_ref, column_ref, parts_ref, cross_ref, row_ref):
    column = 1.0 / jnp.sum(mass_ref[...], axis=0)
    column_ref[...] = column
    scaled_rows(column, weights_ref, parts_ref, scores_ref, cross_ref)

    def put_mass(g, row):
        row_ref[g : g + 1, :] = row

    def put_cross(g, row):
        row_ref[ROW_TILES + g : ROW_TILES + g + 1, :] = row

    row_of_lane_sums(parts_ref, put_mass)
    row_of_lane_sums(cross_ref, put_cross)
    flat, cross = flat_row(row_ref[0:ROW_TILES, :]), row_ref[ROW_TILES : 2 * ROW_TILES, :]
    for k in range(PROTOS):
        pay_ref[k, :, 0:ROWS] = flat
        pay_ref[k, :, ROWS:FLAT] = owned_piece(cross, k)


def column_kernel(gather, mass_ref, weights_ref, pay_ref, extra_ref, scale_ref, sums_ref):
    sums = jnp.sum(mass_ref[...], axis=0)
    column_of_row(1.0 / flat_rows(sums), scale_ref)
    if gather:
        lane = lax.broadcasted_iota(jnp.int32, (1, LANES), 1)
        for g in range(ROW_TILES):
            row = jnp.zeros((1, LANES), f32)
            for t in range(4):
                piece = jnp.where(lane < OWN, mass_ref[(4 * (g % 2) + t) * XS + g // 2, :, ROWS:FLAT], 0.0)
                row = row + (pltpu.roll(piece, t * OWN, 1) if t else piece)
            extra_ref[g : g + 1, :] = row
    else:
        extra_ref[...] = sums[:, ROWS:FLAT]

    sums = [jnp.zeros((8, LANES), f32)] * COL_TILES
    for i in range(0, ROWS, 8):
        rows = pl.ds(i, 8)
        scale = scale_ref[rows, :]
        for t in range(COL_TILES):
            sums[t] = sums[t] + weights_ref[rows, pl.ds(t * LANES, LANES)] * scale
    for t in range(COL_TILES):
        sums_ref[t : t + 1, :] = jnp.sum(sums[t], axis=0, keepdims=True)
    row = sums_ref[...]
    for k in range(BATCHES):
        pay_ref[k] = row


def grad_columns(half, weights_ref, exp_ref, column_ref, unit_t_ref, proto_ref, inverse_ref, prob_ref, target_ref, outs):
    kept_ref, sent_ref = outs
    blocks = [pl.multiple_of(block_rows(p) * 32, 32) for p in range(8)]
    for j in range(0, HALF, CHUNK):
        cols = pl.ds(half * HALF + j, CHUNK)
        pieces = []
        for t in range(half * HALF + j, half * HALF + j + CHUNK, LANES):
            part = pl.ds(t, LANES)
            scale = column_ref[t // LANES : t // LANES + 1, :]
            pieces.append(
                (exp_ref[:, part] * prob_ref[...] - weights_ref[:, part] * scale * target_ref[...]).astype(bf16)
            )
        score_grad = jnp.concatenate(pieces, axis=1)
        grad = jnp.dot(unit_t_ref[...], score_grad, preferred_element_type=f32)
        inverse = inverse_ref[:, cols]
        directions = jnp.concatenate([proto_ref[pl.ds(b, 32), cols] for b in blocks], axis=0) * inverse
        radial = jnp.sum(directions * grad, axis=0, keepdims=True)
        full = (grad - directions * radial) * inverse
        for s in range(4):
            kept_ref[s, :, pl.ds(j, CHUNK)] = full[s * 32 : s * 32 + 32, :]
            sent_ref[s, :, pl.ds(j, CHUNK)] = full[128 + s * 32 : 160 + s * 32, :]


def first_grad_kernel(
    mass_ref,
    total_ref,
    weights_ref,
    exp_ref,
    column_ref,
    unit_t_ref,
    proto_ref,
    inverse_ref,
    kept_ref,
    sent_ref,
    prob_ref,
    target_ref,
    own_ref,
    row_ref,
):
    sums = jnp.sum(mass_ref[...], axis=0)
    row_ref[...] = 1.0 / flat_rows(sums)
    factor = 1.0 / (student_temp * ROWS * BATCHES)
    column_of_row(factor / total_ref[...], prob_ref)
    column_of_row(factor * row_ref[...], target_ref)
    z = lax.axis_index("z")
    line, turn = pl.ds(2 * lax.axis_index("x") + z // 4, 1), LANES - lax.rem(z, 4) * OWN
    row_scale = pltpu.roll(row_ref[line, :], turn, 1)
    total = pltpu.roll(total_ref[line, :], turn, 1)
    own_ref[...] = jnp.log(total) - sums[:, ROWS:FLAT] * row_scale * (1.0 / student_temp)
    tables = (weights_ref, exp_ref, column_ref, unit_t_ref, proto_ref, inverse_ref)
    grad_columns(0, *tables, prob_ref, target_ref, (kept_ref, sent_ref))


def second_grad_kernel(*refs):
    grad_columns(1, *refs[:8], refs[8:])


def pair_kernel(kept_ref, came_ref, own_ref, *out_refs):
    for s, out_ref in zip((2, 1, 3), out_refs):
        exponents = []
        for t in range(HALF // LANES):
            cols = pl.ds(t * LANES, LANES)
            value = kept_ref[s, :, cols] + came_ref[s, :, cols]
            top = jnp.max(jnp.abs(value), axis=0, keepdims=True)
            exponent = jnp.clip(jnp.ceil(jnp.log2(top)), -100.0, 120.0)
            out_ref[:, cols] = value * jnp.exp2(HEAD - exponent)
            exponents.append(exponent)
        out_ref[0:8, HALF:] = jnp.concatenate(exponents, axis=0)
        out_ref[8:32, HALF:] = jnp.zeros((24, LANES), f32)
    own_ref[...] = kept_ref[0] + came_ref[0]


def sum_kernel(*refs):
    out_ref = refs[-1]
    for half in range(2):
        own_ref, *block_refs = refs[4 * half : 4 * half + 4]
        scales = [jnp.exp2(ref[0:8, HALF:] - HEAD) for ref in block_refs]
        for t in range(HALF // LANES):
            cols = pl.ds(t * LANES, LANES)
            value = own_ref[:, cols]
            for ref, scale in zip(block_refs, scales):
                value = value + ref[:, cols] * scale[t : t + 1, :]
            out_ref[:, pl.ds(half * HALF + t * LANES, LANES)] = value


def call(kernel, outs, scratch, homes):
    spaces = {"v": pltpu.VMEM, "h": pltpu.HBM}

    def shape(out):
        dims, dtype, kept = out
        return pltpu.VMEM(dims, dtype) if kept else jax.ShapeDtypeStruct(dims, dtype)

    def run(*operands):
        placed = [
            pltpu.with_memory_space_constraint(x, spaces[h]) if h in spaces else x for x, h in zip(operands, homes)
        ]
        return pl.pallas_call(
            kernel,
            out_shape=[shape(o) for o in outs],
            in_specs=[pl.BlockSpec(memory_space=pl.ANY if h == "h" else pltpu.VMEM) for h in homes],
            out_specs=[pl.BlockSpec(memory_space=pltpu.VMEM if o[2] is not None else pl.ANY) for o in outs],
            scratch_shapes=scratch,
            compiler_params=pltpu.CompilerParams(vmem_limit_bytes=12 * 2**20),
            cost_estimate=pl.CostEstimate(flops=0, bytes_accessed=0, transcendentals=0),
        )(*placed)

    return run


def share(value, axes, count):
    return lax.all_to_all(value, axes, 0, 0, tiled=True)


def shift(value, step, axis="y"):
    return lax.ppermute(value, axis, [(i, (i + step) % 4) for i in range(4)])


def scatter_half(kept, sent):
    came = lax.ppermute(sent, "core", [(0, 1), (1, 0)])
    out = ((32, HALF + LANES), f32, True)
    own, *blocks = call(pair_kernel, [((32, HALF), f32, True), out, out, out], [], "vv")(kept, came)
    return [own] + [shift(block.astype(jnp.float16), k).astype(f32) for block, k in zip(blocks, (2, 1, 3))]


def on_device(student_codes, teacher_codes, prototypes):
    table, column = ((ROWS, COLS), f32, True), ((COL_TILES, LANES), f32, True)
    to_batch, to_proto = ((BATCHES, COL_TILES, LANES), f32, True), ((PROTOS, 1, FLAT), f32, True)
    crops, owned = ((ROW_TILES, LANES), f32, True), ((1, LANES), f32, True)
    lanes, row = pltpu.VMEM((ROWS, LANES), f32), pltpu.VMEM((ROW_TILES, LANES), f32)
    (pay,) = call(
        copy_kernel,
        [((ZS, 2 * OWN, WIDTH), bf16, True)],
        [pltpu.VMEM((2, OWN, WIDTH), bf16), pltpu.SemaphoreType.DMA((2,))],
        "hh",
    )(teacher_codes, student_codes)
    block, inverse_row = ((BLOCK, WIDTH), bf16, True), ((1, COLS), f32, True)
    teacher, student = call(split_kernel, [block, block], [], "v")(share(pay, "z", ZS))
    low, inverse, protos = call(
        norm_kernel,
        [((WIDTH, COLS), bf16, True), inverse_row, ((WIDTH, COLS), f32, True)],
        [pltpu.SemaphoreType.DMA((COLS // WIDE,))],
        "hv",
    )(prototypes, teacher)
    teachers = [teacher] + [shift(teacher, k, "x") for k in (1, 2, 3)]
    above = shift(student, 3, "x")
    students = [student, shift(student, 1, "x"), shift(above, 3, "x"), above]
    weights, mass = call(teacher_kernel, [table, inverse_row], [], "vvvvv")(*teachers, low)
    scores, grown, unit_t, extra, pay = call(
        student_kernel, [table, table, ((WIDTH, ROWS), bf16, True), crops, to_batch], [lanes], "vvvvvv"
    )(*students, low, mass)
    for iteration in range(ITERS - 1):
        first = iteration == 0
        (pay,) = call(functools.partial(row_kernel, first), [to_proto], [lanes, row], "vvv")(
            share(pay, BATCH, BATCHES), weights, extra
        )
        pay, extra = call(
            functools.partial(column_kernel, not first),
            [to_batch, owned if first else crops],
            [lanes, pltpu.VMEM((COL_TILES, LANES), f32)],
            "vv",
        )(share(pay, PROTO, PROTOS), weights)
    pay, column_scale = call(
        last_row_kernel,
        [to_proto, column],
        [lanes, lanes, pltpu.VMEM((2 * ROW_TILES, LANES), f32)],
        "vvv",
    )(share(pay, BATCH, BATCHES), weights, scores)
    part, whole = ((4, 32, HALF), f32, True), ((ROWS, LANES), f32, True)
    tables = (weights, grown, column_scale, unit_t, protos, inverse)
    kept, sent, prob, target, own = call(
        first_grad_kernel, [part, part, whole, whole, ((1, LANES), f32, False)], [row], "vvvvvvvv"
    )(share(pay, PROTO, PROTOS), extra, *tables)
    first = scatter_half(kept, sent)
    kept, sent = call(second_grad_kernel, [part, part], [], "vvvvvvvv")(*tables, prob, target)
    second = scatter_half(kept, sent)
    (out,) = call(sum_kernel, [((32, COLS), f32, False)], [], "vvvvvvvv")(*first, *second)
    return (out, own[0, :OWN])


def solution(mesh):
    fine = Mesh(mesh.devices.reshape(4, 2, 8, 4), BATCH + PROTO)
    rows = P(BATCH + PROTO, None)
    return jax.shard_map(
        on_device,
        mesh=fine,
        in_specs=(rows, rows, P(None, PROTO)),
        out_specs=(P(BATCH, PROTO), P(BATCH + PROTO)),
        check_vma=False,
    )
```

```python
import functools

import jax
import jax.numpy as jnp
from jax import lax
from jax.experimental import pallas as pl
from jax.experimental.pallas import tpu as pltpu
from jax.sharding import Mesh, PartitionSpec as P

ITERS = 3

student_temp = 0.1
teacher_temp = 0.07
norm_eps = 1e-06
log2_e = 1.4426950408889634

BATCH = ("y", "core")
PROTO = ("z", "x")
BATCHES = 8
PROTOS = 32
ROWS = 1024
COLS = 2048
WIDTH = 256
LANES = 128
ROW_TILES = ROWS // LANES
COL_TILES = COLS // LANES
CHUNK = 256
WIDE = 512
HALF = COLS // 2
HEAD = 14.0
FLAT = ROWS + LANES
OWN = ROWS // PROTOS
ZS = 8
XS = 4
BLOCK = ROWS // XS
f32 = jnp.float32
bf16 = jnp.bfloat16


def unit_rows(values):
    values = values.astype(f32)
    return values * lax.rsqrt(jnp.sum(values * values, axis=-1, keepdims=True) + norm_eps)


def row_of_lane_sums(parts_ref, out_row, pieces=ROW_TILES):
    for g in range(pieces):
        block = parts_ref[pl.ds(g * LANES, LANES), :]
        out_row(g, jnp.sum(block.T, axis=0, keepdims=True))


def column_of_row(row, out_ref):
    for g in range(ROW_TILES):
        out_ref[pl.ds(g * LANES, LANES), :] = jnp.broadcast_to(row[g : g + 1, :], (LANES, LANES)).T


def spread_columns(column_mass, pay_ref):
    row = jnp.concatenate([column_mass[:, t * LANES : (t + 1) * LANES] for t in range(COL_TILES)], axis=0)
    for k in range(BATCHES):
        pay_ref[k] = row


def block_place(q):
    step = lax.rem(q // 2 - lax.axis_index("y") + 4, 4)
    return jnp.where(lax.axis_index("core") == q % 2, 0, 4) + step


def block_rows(p):
    row = lax.rem(lax.axis_index("y") + p % 4, 4)
    core = lax.axis_index("core")
    return 2 * row + (core if p < 4 else 1 - core)


def owned_piece(row, k):
    z, x = k // XS, k % XS
    line = 2 * x + z // 4
    return pltpu.roll(row[line : line + 1, :], (LANES - (z % 4) * OWN) % LANES, 1)


def flat_row(row):
    return jnp.concatenate([row[g : g + 1, :] for g in range(ROW_TILES)], axis=1)


def flat_rows(flat):
    return jnp.concatenate([flat[:, g * LANES : (g + 1) * LANES] for g in range(ROW_TILES)], axis=0)


def copy_kernel(teacher_hbm, student_hbm, pay_ref, codes_ref, sems):
    copies = [
        pltpu.make_async_copy(teacher_hbm, codes_ref.at[0], sems.at[0]),
        pltpu.make_async_copy(student_hbm, codes_ref.at[1], sems.at[1]),
    ]
    for copy in copies:
        copy.start()
    for copy in copies:
        copy.wait()
    for t in range(2):
        unit = unit_rows(codes_ref[t]).astype(bf16)
        for k in range(ZS):
            pay_ref[k, pl.ds(t * OWN, OWN), :] = unit


def split_kernel(came_ref, teacher_ref, student_ref):
    teacher_ref[...] = came_ref[:, 0:OWN, :].reshape(BLOCK, WIDTH)
    student_ref[...] = came_ref[:, OWN : 2 * OWN, :].reshape(BLOCK, WIDTH)


def norm_kernel(proto_hbm, after_ref, low_ref, inverse_ref, proto_ref, sems):
    copies = [
        pltpu.make_async_copy(proto_hbm.at[:, pl.ds(j, WIDE)], proto_ref.at[:, pl.ds(j, WIDE)], sems.at[j // WIDE])
        for j in range(0, COLS, WIDE)
    ]
    for copy in copies:
        copy.start()
    for j in range(0, COLS, WIDE):
        copies[j // WIDE].wait()
        cols = pl.ds(j, WIDE)
        piece = proto_ref[:, cols]
        inverse = lax.rsqrt(jnp.sum(piece * piece, axis=0, keepdims=True) + norm_eps)
        inverse_ref[:, cols] = inverse
        low_ref[:, cols] = (piece * inverse).astype(bf16)


def block_starts():
    x = lax.axis_index("x")
    return [pl.multiple_of(lax.rem(x + XS - k, XS) * BLOCK, BLOCK) for k in range(XS)]


def teacher_kernel(u0_ref, u1_ref, u2_ref, u3_ref, low_ref, weights_ref, mass_ref):
    units, starts = (u0_ref, u1_ref, u2_ref, u3_ref), block_starts()

    for j in range(0, COLS, WIDE):
        cols = pl.ds(j, WIDE)
        low = low_ref[:, cols]
        mass = jnp.zeros((8, WIDE), f32)
        for unit_ref, start in zip(units, starts):
            scores = jnp.dot(unit_ref[...], low, preferred_element_type=f32)
            weights = jnp.exp2(scores * (log2_e / teacher_temp))
            weights_ref[pl.ds(start, BLOCK), cols] = weights
            mass = mass + jnp.sum(weights.reshape(BLOCK // 8, 8, WIDE), axis=0)
        mass_ref[:, cols] = jnp.sum(mass, axis=0, keepdims=True)


def student_kernel(
    u0_ref,
    u1_ref,
    u2_ref,
    u3_ref,
    low_ref,
    mass_ref,
    weights_ref,
    product_ref,
    exp_ref,
    unit_t_ref,
    total_ref,
    pay_ref,
    parts_ref,
):
    units, starts = (u0_ref, u1_ref, u2_ref, u3_ref), block_starts()
    place = [pl.multiple_of(block_place(q) * 32, 32) for q in range(8)]
    for unit_ref, start in zip(units, starts):
        turned = unit_ref[...].astype(f32).T.astype(bf16)
        for q in range(8):
            unit_t_ref[pl.ds(place[q], 32), pl.ds(start, BLOCK)] = turned[q * 32 : q * 32 + 32, :]
    parts_ref[...] = jnp.zeros_like(parts_ref)

    for j in range(0, COLS, WIDE):
        cols = pl.ds(j, WIDE)
        low = low_ref[:, cols]
        for unit_ref, start in zip(units, starts):
            rows = pl.ds(start, BLOCK)
            scores = jnp.dot(unit_ref[...], low, preferred_element_type=f32)
            product_ref[rows, cols] = weights_ref[rows, cols] * scores
            grown = jnp.exp2(scores * (log2_e / student_temp))
            exp_ref[rows, cols] = grown
            parts_ref[rows, :] += sum(grown[:, t : t + LANES] for t in range(LANES, WIDE, LANES)) + grown[:, :LANES]

    spread_columns(mass_ref[...], pay_ref)

    def put(g, row):
        total_ref[g : g + 1, :] = row

    row_of_lane_sums(parts_ref, put)


def scaled_rows(column, weights_ref, parts_ref, product_ref=None, cross_ref=None):
    scale = [jnp.broadcast_to(column[t : t + 1, :], (8, LANES)) for t in range(COL_TILES)]

    for i in range(0, ROWS, 8):
        rows = pl.ds(i, 8)
        mass = cross = None
        for t in range(COL_TILES):
            cols = pl.ds(t * LANES, LANES)
            term = weights_ref[rows, cols] * scale[t]
            mass = term if mass is None else mass + term
            if product_ref is not None:
                term = product_ref[rows, cols] * scale[t]
                cross = term if cross is None else cross + term
        parts_ref[rows, :] = mass
        if product_ref is not None:
            cross_ref[rows, :] = cross


def row_kernel(spread, mass_ref, weights_ref, extra_ref, pay_ref, parts_ref, row_ref):
    scaled_rows(1.0 / jnp.sum(mass_ref[...], axis=0), weights_ref, parts_ref)

    def put(g, row):
        row_ref[g : g + 1, :] = row

    row_of_lane_sums(parts_ref, put)
    flat, extra = flat_row(row_ref[...]), extra_ref[...]
    for k in range(PROTOS):
        pay_ref[k, :, 0:ROWS] = flat
        pay_ref[k, :, ROWS:FLAT] = owned_piece(extra, k) if spread else extra


def last_row_kernel(mass_ref, weights_ref, product_ref, pay_ref, column_ref, parts_ref, cross_ref, row_ref):
    column = 1.0 / jnp.sum(mass_ref[...], axis=0)
    column_ref[...] = column
    scaled_rows(column, weights_ref, parts_ref, product_ref, cross_ref)

    def put_mass(g, row):
        row_ref[g : g + 1, :] = row

    def put_cross(g, row):
        row_ref[ROW_TILES + g : ROW_TILES + g + 1, :] = row

    row_of_lane_sums(parts_ref, put_mass)
    row_of_lane_sums(cross_ref, put_cross)
    flat, cross = flat_row(row_ref[0:ROW_TILES, :]), row_ref[ROW_TILES : 2 * ROW_TILES, :]
    for k in range(PROTOS):
        pay_ref[k, :, 0:ROWS] = flat
        pay_ref[k, :, ROWS:FLAT] = owned_piece(cross, k)


def column_kernel(gather, mass_ref, weights_ref, pay_ref, extra_ref, scale_ref, sums_ref):
    sums = jnp.sum(mass_ref[...], axis=0)
    column_of_row(1.0 / flat_rows(sums), scale_ref)
    if gather:
        lane = lax.broadcasted_iota(jnp.int32, (1, LANES), 1)
        for g in range(ROW_TILES):
            row = jnp.zeros((1, LANES), f32)
            for t in range(4):
                piece = jnp.where(lane < OWN, mass_ref[(4 * (g % 2) + t) * XS + g // 2, :, ROWS:FLAT], 0.0)
                row = row + (pltpu.roll(piece, t * OWN, 1) if t else piece)
            extra_ref[g : g + 1, :] = row
    else:
        extra_ref[...] = sums[:, ROWS:FLAT]

    sums = [jnp.zeros((8, LANES), f32)] * COL_TILES
    for i in range(0, ROWS, 8):
        rows = pl.ds(i, 8)
        scale = scale_ref[rows, :]
        for t in range(COL_TILES):
            sums[t] = sums[t] + weights_ref[rows, pl.ds(t * LANES, LANES)] * scale
    for t in range(COL_TILES):
        sums_ref[t : t + 1, :] = jnp.sum(sums[t], axis=0, keepdims=True)
    row = sums_ref[...]
    for k in range(BATCHES):
        pay_ref[k] = row


def grad_columns(half, weights_ref, exp_ref, column_ref, unit_t_ref, proto_ref, inverse_ref, prob_ref, target_ref, outs):
    kept_ref, sent_ref = outs
    blocks = [pl.multiple_of(block_rows(p) * 32, 32) for p in range(8)]
    for j in range(0, HALF, CHUNK):
        cols = pl.ds(half * HALF + j, CHUNK)
        pieces = []
        for t in range(half * HALF + j, half * HALF + j + CHUNK, LANES):
            part = pl.ds(t, LANES)
            scale = column_ref[t // LANES : t // LANES + 1, :]
            pieces.append(
                (exp_ref[:, part] * prob_ref[...] - weights_ref[:, part] * scale * target_ref[...]).astype(bf16)
            )
        score_grad = jnp.concatenate(pieces, axis=1)
        grad = jnp.dot(unit_t_ref[...], score_grad, preferred_element_type=f32)
        inverse = inverse_ref[:, cols]
        directions = jnp.concatenate([proto_ref[pl.ds(b, 32), cols] for b in blocks], axis=0) * inverse
        radial = jnp.sum(directions * grad, axis=0, keepdims=True)
        full = (grad - directions * radial) * inverse
        for s in range(4):
            kept_ref[s, :, pl.ds(j, CHUNK)] = full[s * 32 : s * 32 + 32, :]
            sent_ref[s, :, pl.ds(j, CHUNK)] = full[128 + s * 32 : 160 + s * 32, :]


def first_grad_kernel(
    mass_ref,
    total_ref,
    weights_ref,
    exp_ref,
    column_ref,
    unit_t_ref,
    proto_ref,
    inverse_ref,
    kept_ref,
    sent_ref,
    prob_ref,
    target_ref,
    own_ref,
    row_ref,
):
    sums = jnp.sum(mass_ref[...], axis=0)
    row_ref[...] = 1.0 / flat_rows(sums)
    factor = 1.0 / (student_temp * ROWS * BATCHES)
    column_of_row(factor / total_ref[...], prob_ref)
    column_of_row(factor * row_ref[...], target_ref)
    z = lax.axis_index("z")
    line, turn = pl.ds(2 * lax.axis_index("x") + z // 4, 1), LANES - lax.rem(z, 4) * OWN
    row_scale = pltpu.roll(row_ref[line, :], turn, 1)
    total = pltpu.roll(total_ref[line, :], turn, 1)
    own_ref[...] = jnp.log(total) - sums[:, ROWS:FLAT] * row_scale * (1.0 / student_temp)
    tables = (weights_ref, exp_ref, column_ref, unit_t_ref, proto_ref, inverse_ref)
    grad_columns(0, *tables, prob_ref, target_ref, (kept_ref, sent_ref))


def second_grad_kernel(*refs):
    grad_columns(1, *refs[:8], refs[8:])


def pair_kernel(kept_ref, came_ref, own_ref, *out_refs):
    for s, out_ref in zip((2, 1, 3), out_refs):
        exponents = []
        for t in range(HALF // LANES):
            cols = pl.ds(t * LANES, LANES)
            value = kept_ref[s, :, cols] + came_ref[s, :, cols]
            top = jnp.max(jnp.abs(value), axis=0, keepdims=True)
            exponent = jnp.clip(jnp.ceil(jnp.log2(top)), -100.0, 120.0)
            out_ref[:, cols] = value * jnp.exp2(HEAD - exponent)
            exponents.append(exponent)
        out_ref[0:8, HALF:] = jnp.concatenate(exponents, axis=0)
        out_ref[8:32, HALF:] = jnp.zeros((24, LANES), f32)
    own_ref[...] = kept_ref[0] + came_ref[0]


def half_sum(own_ref, block_refs, out_ref):
    scales = [jnp.exp2(ref[0:8, HALF:] - HEAD) for ref in block_refs]
    for t in range(HALF // LANES):
        cols = pl.ds(t * LANES, LANES)
        value = own_ref[:, cols]
        for ref, scale in zip(block_refs, scales):
            value = value + ref[:, cols] * scale[t : t + 1, :]
        out_ref[:, cols] = value


def sum_kernel(own_ref, *refs):
    half_sum(own_ref, refs[:3], refs[3])


def last_sum_kernel(first_ref, own_ref, *refs):
    out_hbm, second_ref, sems = refs[3:]
    copies = [
        pltpu.make_async_copy(ref, out_hbm.at[:, pl.ds(half * HALF, HALF)], sems.at[half])
        for half, ref in enumerate((first_ref, second_ref))
    ]
    copies[0].start()
    half_sum(own_ref, refs[:3], second_ref)
    copies[1].start()
    for copy in copies:
        copy.wait()


def call(kernel, outs, scratch, homes):
    spaces = {"v": pltpu.VMEM, "h": pltpu.HBM}

    def shape(out):
        dims, dtype, kept = out
        return pltpu.VMEM(dims, dtype) if kept else jax.ShapeDtypeStruct(dims, dtype)

    def run(*operands):
        placed = [
            pltpu.with_memory_space_constraint(x, spaces[h]) if h in spaces else x for x, h in zip(operands, homes)
        ]
        return pl.pallas_call(
            kernel,
            out_shape=[shape(o) for o in outs],
            in_specs=[pl.BlockSpec(memory_space=pl.ANY if h == "h" else pltpu.VMEM) for h in homes],
            out_specs=[pl.BlockSpec(memory_space=pltpu.VMEM if o[2] is not None else pl.ANY) for o in outs],
            scratch_shapes=scratch,
            compiler_params=pltpu.CompilerParams(vmem_limit_bytes=12 * 2**20),
            cost_estimate=pl.CostEstimate(flops=0, bytes_accessed=0, transcendentals=0),
        )(*placed)

    return run


def share(value, axes, count):
    return lax.all_to_all(value, axes, 0, 0, tiled=True)


def shift(value, step, axis="y"):
    return lax.ppermute(value, axis, [(i, (i + step) % 4) for i in range(4)])


def scatter_half(kept, sent):
    came = lax.ppermute(sent, "core", [(0, 1), (1, 0)])
    out = ((32, HALF + LANES), f32, True)
    own, *blocks = call(pair_kernel, [((32, HALF), f32, True), out, out, out], [], "vv")(kept, came)
    return [own] + [shift(block.astype(jnp.float16), k).astype(f32) for block, k in zip(blocks, (2, 1, 3))]


def on_device(student_codes, teacher_codes, prototypes):
    table, column = ((ROWS, COLS), f32, True), ((COL_TILES, LANES), f32, True)
    to_batch, to_proto = ((BATCHES, COL_TILES, LANES), f32, True), ((PROTOS, 1, FLAT), f32, True)
    crops, owned = ((ROW_TILES, LANES), f32, True), ((1, LANES), f32, True)
    lanes, row = pltpu.VMEM((ROWS, LANES), f32), pltpu.VMEM((ROW_TILES, LANES), f32)
    (pay,) = call(
        copy_kernel,
        [((ZS, 2 * OWN, WIDTH), bf16, True)],
        [pltpu.VMEM((2, OWN, WIDTH), bf16), pltpu.SemaphoreType.DMA((2,))],
        "hh",
    )(teacher_codes, student_codes)
    block, inverse_row = ((BLOCK, WIDTH), bf16, True), ((1, COLS), f32, True)
    teacher, student = call(split_kernel, [block, block], [], "v")(share(pay, "z", ZS))
    low, inverse, protos = call(
        norm_kernel,
        [((WIDTH, COLS), bf16, True), inverse_row, ((WIDTH, COLS), f32, True)],
        [pltpu.SemaphoreType.DMA((COLS // WIDE,))],
        "hv",
    )(prototypes, teacher)
    teachers = [teacher] + [shift(teacher, k, "x") for k in (1, 2, 3)]
    above = shift(student, 3, "x")
    students = [student, shift(student, 1, "x"), shift(above, 3, "x"), above]
    weights, mass = call(teacher_kernel, [table, inverse_row], [], "vvvvv")(*teachers, low)
    product, grown, unit_t, extra, pay = call(
        student_kernel, [table, table, ((WIDTH, ROWS), bf16, True), crops, to_batch], [lanes], "vvvvvvv"
    )(*students, low, mass, weights)
    for iteration in range(ITERS - 1):
        first = iteration == 0
        (pay,) = call(functools.partial(row_kernel, first), [to_proto], [lanes, row], "vvv")(
            share(pay, BATCH, BATCHES), weights, extra
        )
        pay, extra = call(
            functools.partial(column_kernel, not first),
            [to_batch, owned if first else crops],
            [lanes, pltpu.VMEM((COL_TILES, LANES), f32)],
            "vv",
        )(share(pay, PROTO, PROTOS), weights)
    pay, column_scale = call(
        last_row_kernel,
        [to_proto, column],
        [lanes, lanes, pltpu.VMEM((2 * ROW_TILES, LANES), f32)],
        "vvv",
    )(share(pay, BATCH, BATCHES), weights, product)
    part, whole = ((4, 32, HALF), f32, True), ((ROWS, LANES), f32, True)
    tables = (weights, grown, column_scale, unit_t, protos, inverse)
    kept, sent, prob, target, own = call(
        first_grad_kernel, [part, part, whole, whole, ((1, LANES), f32, False)], [row], "vvvvvvvv"
    )(share(pay, PROTO, PROTOS), extra, *tables)
    first = scatter_half(kept, sent)
    kept, sent = call(second_grad_kernel, [part, part], [], "vvvvvvvv")(*tables, prob, target)
    second = scatter_half(kept, sent)
    half = ((32, HALF), f32, True)
    (first,) = call(sum_kernel, [half], [], "vvvv")(*first)
    (out,) = call(
        last_sum_kernel,
        [((32, COLS), f32, None)],
        [pltpu.VMEM((32, HALF), f32), pltpu.SemaphoreType.DMA((2,))],
        "vvvvv",
    )(first, *second)
    return (out, own[0, :OWN])


def solution(mesh):
    fine = Mesh(mesh.devices.reshape(4, 2, 8, 4), BATCH + PROTO)
    rows = P(BATCH + PROTO, None)
    return jax.shard_map(
        on_device,
        mesh=fine,
        in_specs=(rows, rows, P(None, PROTO)),
        out_specs=(P(BATCH, PROTO), P(BATCH + PROTO)),
        check_vma=False,
    )
```
